512 devices in a mesh: ctx: 64 (over z_hi, y, core), tp: 8 (over x, z_lo).
Axes of the slice: x: 4, y: 8, z: 8 (z_hi: 4, z_lo: 2; z = z_hi * 2 + z_lo), core: 2. Of those that a mesh axis runs over, the one named last changes fastest.
Arguments:
- x_stash: bfloat16 [8192, 4096], P('ctx', 'tp'), may hold values from -6 to 6
- w_key: bfloat16 [4096, 1024], P(None, 'tp'), may hold values from -0.09375 to 0.09375
- w_value: bfloat16 [4096, 1024], P(None, 'tp'), may hold values from -0.09375 to 0.09375
- query: bfloat16 [8192, 4096], P('ctx', 'tp'), may hold values from -64 to 64
- out_stash: bfloat16 [8192, 4096], P('ctx', 'tp'), may hold values from -6 to 6
- d_out: bfloat16 [8192, 4096], P('ctx', 'tp'), may hold values from -24 to 24
- roster: int32 [128], replicated, may hold values from 0 to 127, each once
Outputs:
- d_query: bfloat16 [8192, 4096], P('ctx', 'tp')
- d_input: bfloat16 [8192, 4096], P('ctx', 'tp')
The draws below stay inside these ranges and needn't reach their ends.
Inputs may be any that keep to these rules, and one draw needn't show every extreme that they name: Every block index of the sequence appears once; stored rows r * 128 to r * 128 + 63 are block roster[2 r], the next 64 rows block roster[2 r + 1].
All inputs are finite; a program needn't handle non-finite values.
Results may differ from the reference program's by a relative error of at most 0.025.
The reference program's roundings to bfloat16 on the way (of `keys`, `probs_b`, `d_scores` and `d_key_b`) count: a program that leaves them out, or rounds other values in their place, can miss the bound.
Values may be sent and summed in bfloat16 or wider, within the bound.
A program may use at most 64 MiB of HBM per device.

```python
import math
import jax
import jax.numpy as jnp
from jax import lax

D = 4096
HD = 128
GROUP = 4
KV_DEV = 1
BLOCK = 64
TOKENS = 8192
KVH = 8
QH = 32
N_CTX = 64
N_TP = 8


def draw_query(key, part):
    key = jax.random.fold_in(key, 11)
    key_base, key_scale = jax.random.split(key, 2)
    shape = (TOKENS, QH, HD)
    row_scale = jnp.exp(jax.random.uniform(key_scale, (TOKENS, QH, 1), jnp.float32, minval=math.log(0.3), maxval=math.log(3.0)))
    drawn = jax.random.normal(key_base, shape, jnp.float32) * row_scale
    return jnp.clip(drawn, -64.0, 64.0).reshape(TOKENS, QH * HD).astype(jnp.bfloat16)


def steps_of(stream_key, shape, cuts, least, largest):
    def one(dim, shards_of):
        draws = jax.random.uniform(jax.random.fold_in(jax.random.fold_in(stream_key, 6), dim), (shards_of,), jnp.float32, least / len(cuts), largest / len(cuts))
        return jnp.repeat(jnp.exp(draws), shape[dim] // shards_of).reshape((-1,) + (1,) * (len(shape) - dim - 1))

    level = one(*cuts[0])
    for cut in cuts[1:]:
        level = level * one(*cut)
    return level


def bell_draw(key, shape, spread, most, pieces=(), held_as=jnp.bfloat16):
    loudness = steps_of(key, shape, pieces, -0.22, 0.18) if pieces else 1.0
    values = jax.random.normal(key, shape, jnp.float32) * spread * loudness
    return jnp.minimum(jnp.maximum(values, -most), most).astype(held_as)


def setup_inputs(seed: int = 0) -> dict:
    splits = jax.random.split(jax.random.key(seed), 8)
    x_stash = bell_draw(splits[0], (TOKENS, D), 1.0, 6.0, ((0, 64), (1, 8)))
    w_key = bell_draw(splits[1], (D, KVH * HD), D ** -0.5, 0.09375, ((1, 8),))
    w_value = bell_draw(splits[2], (D, KVH * HD), D ** -0.5, 0.09375, ((1, 8),))
    query = draw_query(jax.random.fold_in(splits[7], 71), 0)
    out_stash = bell_draw(splits[4], (TOKENS, QH * HD), 1.0, 6.0, ((0, 64), (1, 8)))
    d_out = bell_draw(splits[5], (TOKENS, QH * HD), 4.0, 24.0, ((0, 64), (1, 8)))
    roster = jax.random.permutation(splits[6], 2 * N_CTX).astype(jnp.int32)
    return dict(x_stash=x_stash, w_key=w_key, w_value=w_value, query=query, out_stash=out_stash, d_out=d_out, roster=roster)


NEG_FILL = -1.0e30
ROPE_BASE = 500000.0


def rope_tables(positions, head_dim):
    half_dim = head_dim // 2
    frequency = ROPE_BASE ** (-(jnp.arange(half_dim, dtype=jnp.float32) * 2.0) / head_dim)
    angles = positions.astype(jnp.float32)[:, None, None] * frequency[None, None, :]
    return jnp.cos(angles), jnp.sin(angles)


def rotate(tensor, cosine, sine_part, direction):
    half_dim = tensor.shape[-1] // 2
    first_half = tensor[..., :half_dim]
    second_half = tensor[..., half_dim:]
    return jnp.concatenate([first_half * cosine - direction * second_half * sine_part,
                            second_half * cosine + direction * first_half * sine_part], axis=-1)


def reference(x_stash, w_key, w_value, query, out_stash, d_out, roster):
    row_ids = jnp.arange(TOKENS, dtype=jnp.int32)
    position = jnp.take(roster, row_ids // BLOCK) * BLOCK + row_ids % BLOCK
    cosine, sine_part = rope_tables(position, HD)
    key_raw = jnp.dot(x_stash, w_key, preferred_element_type=jnp.float32).reshape(TOKENS, KVH, HD)
    value_raw = jnp.dot(x_stash, w_value, preferred_element_type=jnp.float32).reshape(TOKENS, KVH, HD)
    keys = rotate(key_raw, cosine, sine_part, 1.0).astype(jnp.bfloat16)
    values = value_raw.astype(jnp.bfloat16)
    allowed = position[None, :] <= position[:, None]
    score_scale = HD ** -0.5
    key_heads = jnp.transpose(keys, (1, 0, 2))
    value_heads = jnp.transpose(values, (1, 0, 2))
    query_heads = jnp.transpose(query.reshape(TOKENS, QH, HD), (1, 0, 2))
    grad_heads = jnp.transpose(d_out.reshape(TOKENS, QH, HD), (1, 0, 2))
    out_heads = jnp.transpose(out_stash.reshape(TOKENS, QH, HD), (1, 0, 2))
    kv_ids = jnp.arange(QH, dtype=jnp.int32) // GROUP

    def one_head(inputs):
        query_head, grad_head, out_head, kv_index = inputs
        key_head = lax.dynamic_index_in_dim(key_heads, kv_index.astype(jnp.int32), 0, keepdims=False)
        value_head = lax.dynamic_index_in_dim(value_heads, kv_index.astype(jnp.int32), 0, keepdims=False)
        scores = jnp.dot(query_head, key_head.T, preferred_element_type=jnp.float32) * score_scale
        masked = jnp.where(allowed, scores, NEG_FILL)
        row_peak = jnp.max(masked, axis=-1)
        exp_total = jnp.sum(jnp.where(allowed, jnp.exp(masked - row_peak[:, None]), 0.0), axis=-1)
        log_total = row_peak + jnp.log(exp_total)
        probs_f = jnp.where(allowed, jnp.exp(scores - log_total[:, None]), 0.0)
        probs_b = probs_f.astype(jnp.bfloat16)
        delta = jnp.sum(grad_head.astype(jnp.float32) * out_head.astype(jnp.float32), axis=-1)
        d_value = jnp.dot(probs_b.T, grad_head, preferred_element_type=jnp.float32)
        d_probs = jnp.dot(grad_head, value_head.T, preferred_element_type=jnp.float32)
        d_scores = (probs_f * (d_probs - delta[:, None])).astype(jnp.bfloat16)
        d_query = jnp.dot(d_scores, key_head, preferred_element_type=jnp.float32) * score_scale
        d_key = jnp.dot(d_scores.T, query_head, preferred_element_type=jnp.float32) * score_scale
        return d_query, d_key, d_value

    d_query, d_key_rot, d_value = lax.map(one_head, (query_heads, grad_heads, out_heads, kv_ids))
    d_query_out = jnp.transpose(d_query, (1, 0, 2)).reshape(TOKENS, QH * HD).astype(jnp.bfloat16)
    d_key_sum = jnp.transpose(jnp.sum(d_key_rot.reshape(KVH, GROUP, TOKENS, HD), axis=1), (1, 0, 2))
    d_value_sum = jnp.transpose(jnp.sum(d_value.reshape(KVH, GROUP, TOKENS, HD), axis=1), (1, 0, 2))
    d_key_b = rotate(d_key_sum, cosine, sine_part, -1.0).astype(jnp.bfloat16).reshape(TOKENS, KVH * HD)
    d_value_b = d_value_sum.astype(jnp.bfloat16).reshape(TOKENS, KVH * HD)
    width_dev = KV_DEV * HD
    d_input = jnp.zeros((TOKENS, D), jnp.float32)
    for device_index in range(N_TP):
        low = device_index * width_dev
        partial_sum = jnp.dot(d_key_b[:, low:low + width_dev], w_key[:, low:low + width_dev].T,
                              preferred_element_type=jnp.float32)
        partial_sum = partial_sum + jnp.dot(d_value_b[:, low:low + width_dev], w_value[:, low:low + width_dev].T,
                                            preferred_element_type=jnp.float32)
        rounded = lax.optimization_barrier(partial_sum.astype(jnp.bfloat16))
        d_input = d_input + rounded.astype(jnp.float32)
    return d_query_out, d_input.astype(jnp.bfloat16)
```

```python
import functools

import jax
import jax.numpy as jnp
import numpy as np
from jax import lax
from jax.experimental import pallas as pl
from jax.experimental.pallas import tpu as pltpu
from jax.sharding import PartitionSpec as P

HD = 128
GROUP = 4
BLOCK = 64
ROWS = 128
WIDE = GROUP * HD
ROPE_BASE = 500000.0
SCALE = HD ** -0.5
LOG2E = 1.4426950408889634
NEG = -1e30
FLOOR = -1e20

GRIDS = {(64, 8): (4, 8, 4, 2)}

NT = (((1,), (1,)), ((), ()))


def matmul_nt(a, b):
    return lax.dot_general(a, b, NT, preferred_element_type=jnp.float32)


def matmul(a, b):
    return jnp.dot(a, b, preferred_element_type=jnp.float32)


def stacked(block):
    return jnp.concatenate([block[:, h * HD:(h + 1) * HD] for h in range(GROUP)], axis=0)


def far_first(count):
    return sorted(range(count), key=lambda d: (-min(d, count - d), d))


def near_first(count):
    return sorted(range(1, count), key=lambda d: (min(d, count - d), d))


def kernel(
    grid, x_in, wk_in, wv_in, q_in, o_in, g_in, roster, freq,
    dq_out, di_out,
    xg, wkv, qg, gg, ol, kv, kt, posk, posq, probs, peak, total, fac, lse_own, lse_got,
    delta, dqt, dq_snd, dq_sib, dq_got, acc, dkv_snd, dkv_got, di_snd, di_got, dq_res, di_res,
    send_sem, recv_sem, local_sem,
):
    nz, ny, nx, nl = grid
    nj = 2 * nz
    chunks = ny // 2
    ctx, tp = lax.axis_index("ctx"), lax.axis_index("tp")
    z, y, c = ctx // (2 * ny), (ctx // 2) % ny, ctx % 2
    xi, zl = tp // nl, tp % nl

    def ctx_at(dz, dy, dc):
        return (((z + dz) % nz) * ny + (y + dy) % ny) * 2 + (c + dc) % 2

    def tp_at(dx, dl):
        return ((xi + dx) % nx) * nl + (zl + dl) % nl

    tp_peers = [(dx, dl) for dx in range(nx) for dl in range(nl) if (dx, dl) != (0, 0)]
    q_peers = [(dz, dc) for dz in range(nz) for dc in range(2) if (dz, dc) != (0, 0)]
    y_peers = list(range(1, ny))

    used = [0, 0]

    def local(src, dst):
        copy = pltpu.make_async_copy(src, dst, local_sem.at[used[0]])
        used[0] += 1
        copy.start()
        return copy

    sent = []

    def remote(src, dst, at_ctx, at_tp):
        i = used[1]
        used[1] += 1
        copy = pltpu.make_async_remote_copy(
            src_ref=src, dst_ref=dst, send_sem=send_sem.at[i], recv_sem=recv_sem.at[i],
            device_id=(at_ctx, at_tp), device_id_type=pl.DeviceIdType.MESH,
        )
        copy.start()
        sent.append(copy)
        return copy

    load_x = local(x_in, xg.at[0])
    load_wk = local(wk_in, wkv.at[:, 0:HD])
    load_wv = local(wv_in, wkv.at[:, HD:2 * HD])
    load_g = local(g_in, gg.at[0])
    load_o = local(o_in, ol)
    load_q = local(q_in, qg.at[0])

    barrier = pltpu.get_barrier_semaphore()
    partners = [(ctx, tp_at(dx, dl)) for dx, dl in tp_peers]
    partners += [(ctx_at(dz, 0, dc), tp) for dz, dc in q_peers]
    partners += [(ctx_at(0, dy, 0), tp) for dy in y_peers]
    for partner in partners:
        pl.semaphore_signal(barrier, inc=1, device_id=partner, device_id_type=pl.DeviceIdType.MESH)
    pl.semaphore_wait(barrier, len(partners))

    got_x = {}
    if nl > 1:
        got_x[0, 1] = remote(x_in, xg.at[1], ctx, tp_at(0, 1))
    for dx in near_first(nx):
        got_x[dx, 0] = remote(x_in, xg.at[dx * nl], ctx, tp_at(dx, 0))
    got_q = {}
    for dz in near_first(nz):
        got_q[dz, 0] = remote(q_in, qg.at[2 * dz], ctx_at(dz, 0, 0), tp)
    got_q[0, 1] = remote(q_in, qg.at[1], ctx_at(0, 0, 1), tp)

    order = far_first(ny)
    place = {dy: p for p, dy in enumerate(order)}
    row_id = lax.broadcasted_iota(jnp.int32, (ROWS, HD), 0)
    lane_id = lax.broadcasted_iota(jnp.int32, (1, ROWS), 1)
    for p, dy in enumerate(order):
        at = ctx_at(0, ny - dy, 0)
        first, second = roster[2 * at] * BLOCK, roster[2 * at + 1] * BLOCK
        posk[p * ROWS:(p + 1) * ROWS, :] = row_id + jnp.where(row_id < BLOCK, first, second - BLOCK)
    for j in range(nj):
        at = ctx_at(nz - j // 2, 0, 2 - j % 2)
        first, second = roster[2 * at] * BLOCK, roster[2 * at + 1] * BLOCK
        posq[j:j + 1, :] = lane_id + jnp.where(lane_id < BLOCK, first, second - BLOCK)
    own = place[0]
    angle = posk[own * ROWS:(own + 1) * ROWS, :].astype(jnp.float32) * freq[...]
    cosine = jnp.cos(angle)
    lane = lax.broadcasted_iota(jnp.int32, (ROWS, HD), 1)
    sine = jnp.where(lane < HD // 2, -1.0, 1.0) * jnp.sin(angle)

    load_g.wait()
    load_o.wait()
    for h in range(GROUP):
        cols = slice(h * HD, (h + 1) * HD)
        product = gg[0, :, cols].astype(jnp.float32) * ol[:, cols].astype(jnp.float32)
        delta[0, :, cols] = jnp.sum(product.T, axis=0, keepdims=True)

    def project(dx, dl):
        at = ((xi + nx - dx) % nx) * nl + (zl + nl - dl) % nl
        rows = pl.ds(pl.multiple_of(at * WIDE, WIDE), WIDE)
        return matmul(xg[dx * nl + dl], wkv[rows, :])

    load_x.wait()
    load_wk.wait()
    load_wv.wait()
    raw = project(0, 0)
    if nl > 1:
        got_x[0, 1].wait_recv()
        for dx in near_first(nx):
            got_x[dx, 1] = remote(xg.at[1], xg.at[dx * nl + 1], ctx, tp_at(dx, 0))
        raw += project(0, 1)
    for dx in near_first(nx):
        got_x[dx, 0].wait_recv()
        raw += project(dx, 0)
    got_g = {}
    for dz in near_first(nz):
        got_g[dz, 0] = remote(g_in, gg.at[2 * dz], ctx_at(dz, 0, 0), tp)
    got_g[0, 1] = remote(g_in, gg.at[1], ctx_at(0, 0, 1), tp)
    got_delta = [
        remote(delta.at[0], delta.at[2 * dz + dc], ctx_at(dz, 0, dc), tp) for dz, dc in q_peers
    ]
    for dz in near_first(nz):
        got_q[dz, 0].wait_recv()
        got_q[dz, 1] = remote(qg.at[2 * dz], qg.at[2 * dz + 1], ctx_at(0, 0, 1), tp)
    if nl > 1:
        for dx in near_first(nx):
            got_x[dx, 1].wait_recv()
            raw += project(dx, 1)
    key_raw = raw[:, 0:HD]
    keys = key_raw * cosine + pltpu.roll(key_raw, HD // 2, 1) * sine
    own_rows = pl.ds(own * ROWS, ROWS)
    kv[own_rows, 0:HD] = keys.astype(jnp.bfloat16)
    kv[own_rows, HD:2 * HD] = raw[:, HD:2 * HD].astype(jnp.bfloat16)
    got_kv = {}
    for dy in near_first(ny):
        got_kv[dy] = remote(
            kv.at[own_rows, :], kv.at[pl.ds(place[dy] * ROWS, ROWS), :], ctx_at(0, dy, 0), tp
        )
    load_q.wait()
    got_q[0, 1].wait_recv()
    for dz in near_first(nz):
        got_q[dz, 1].wait_recv()

    def table_row(j):
        at = ((z + nz - j // 2) % nz) * 2 + (c + 2 - j % 2) % 2
        return at

    for k in reversed(range(chunks)):
        for dy in order[2 * k:2 * k + 2]:
            if dy:
                got_kv[dy].wait_recv()
        rows = slice(2 * k * ROWS, 2 * (k + 1) * ROWS)
        kt[k] = kv[rows, 0:HD].astype(jnp.float32).T.astype(jnp.bfloat16)

        def score_step(j, carry, k=k, rows=rows):
            at = table_row(j)
            scores = matmul_nt(kv[rows, 0:HD], stacked(qg[j]))
            allowed = posk[rows, :] <= posq[pl.ds(j, 1), :]
            for h in range(GROUP):
                cols = slice(h * HD, (h + 1) * HD)
                part = jnp.where(allowed, scores[:, cols] * (SCALE * LOG2E), NEG)
                top = jnp.maximum(jnp.max(part, axis=0, keepdims=True), FLOOR)
                weight = jnp.exp2(part - top)
                probs[k, j, :, cols] = weight
                peak[k, at, :, cols] = top
                total[k, at, :, cols] = jnp.sum(weight, axis=0, keepdims=True)
            return carry

        lax.fori_loop(0, nj, score_step, 0)

    top = peak[0]
    for k in range(1, chunks):
        top = jnp.maximum(top, peak[k])
    mass = total[0] * jnp.exp2(peak[0] - top)
    for k in range(1, chunks):
        mass += total[k] * jnp.exp2(peak[k] - top)
    lse_own[...] = jnp.where(mass > 0.0, top + jnp.log(jnp.maximum(mass, 1e-30)) * LOG2E, NEG)
    got_lse = [
        remote(lse_own, lse_got.at[2 * dz + dc], ctx_at(dz, 0, dc), tp) for dz, dc in q_peers
    ]
    load_g_sib = got_g[0, 1]
    for dz in near_first(nz):
        got_g[dz, 0].wait_recv()
        got_g[dz, 1] = remote(gg.at[2 * dz], gg.at[2 * dz + 1], ctx_at(0, 0, 1), tp)
    for copy in got_lse:
        copy.wait_recv()
    top = lse_own[...]
    for s in range(1, nj):
        top = jnp.maximum(top, lse_got[s])
    mass = jnp.exp2(lse_own[...] - top)
    for s in range(1, nj):
        mass += jnp.exp2(lse_got[s] - top)
    lse = top + jnp.log(mass) * LOG2E
    for k in range(chunks):
        fac[k] = jnp.exp2(peak[k] - lse)
    for copy in got_delta:
        copy.wait_recv()
    load_g_sib.wait_recv()
    for dz in near_first(nz):
        got_g[dz, 1].wait_recv()

    got_dkv = {}
    got_sib = {}
    for k in range(chunks):
        rows = slice(2 * k * ROWS, 2 * (k + 1) * ROWS)
        acc[...] = jnp.zeros_like(acc)

        def grad_step(j, k=k, rows=rows):
            at = table_row(j)
            gs, qs = stacked(gg[j]), stacked(qg[j])
            d_probs = matmul_nt(kv[rows, HD:2 * HD], gs)
            prob = probs[k, j] * fac[k, at]
            d_scores = (prob * (d_probs - delta[j])).astype(jnp.bfloat16)
            acc[:, HD:2 * HD] += matmul(prob.astype(jnp.bfloat16), gs)
            acc[:, 0:HD] += matmul(d_scores, qs)
            part = matmul(kt[k], d_scores)
            if k == 0:
                dqt[j] = part
            else:
                dqt[j] += part

        def odd(i, carry, step=grad_step):
            step(2 * i + 1)
            return carry

        def even(i, carry, step=grad_step):
            step(2 * i)
            return carry

        def every(j, carry, step=grad_step):
            step(j)
            return carry

        if k < chunks - 1:
            lax.fori_loop(0, nj, every, 0)
        else:
            lax.fori_loop(0, nz, odd, 0)
            for dz in range(nz):
                dq_snd[dz] = (dqt[2 * dz + 1] * SCALE).astype(jnp.bfloat16)
                got_sib[dz] = remote(dq_snd.at[dz], dq_sib.at[dz], ctx_at(0, 0, 1), tp)
            lax.fori_loop(0, nz, even, 0)
        for i, dy in enumerate(order[2 * k:2 * k + 2]):
            if dy == 0:
                continue
            p = 2 * k + i
            part = acc[i * ROWS:(i + 1) * ROWS, :]
            dkv_snd[p, :, 0:HD] = (part[:, 0:HD] * SCALE).astype(jnp.bfloat16)
            dkv_snd[p, :, HD:2 * HD] = part[:, HD:2 * HD].astype(jnp.bfloat16)
            got_dkv[dy] = remote(dkv_snd.at[p], dkv_got.at[p], ctx_at(0, ny - dy, 0), tp)

    got_dq = {}
    for dz in far_first(nz):
        if dz:
            got_sib[dz].wait_recv()
            both = dqt[2 * dz] * SCALE + dq_sib[dz].astype(jnp.float32)
            dq_snd[nz + dz] = both.astype(jnp.bfloat16)
            got_dq[dz] = remote(dq_snd.at[nz + dz], dq_got.at[dz], ctx_at(nz - dz, 0, 0), tp)

    i = own % 2
    d_key = acc[i * ROWS:(i + 1) * ROWS, 0:HD] * SCALE
    d_value = acc[i * ROWS:(i + 1) * ROWS, HD:2 * HD]
    for dy in order:
        if dy:
            got_dkv[dy].wait_recv()
            d_key += dkv_got[place[dy], :, 0:HD].astype(jnp.float32)
            d_value += dkv_got[place[dy], :, HD:2 * HD].astype(jnp.float32)
    d_key = d_key * cosine - pltpu.roll(d_key, HD // 2, 1) * sine
    d_kv = jnp.concatenate([d_key, d_value], axis=1).astype(jnp.bfloat16)

    def term(dx, dl):
        rows = pl.ds(pl.multiple_of(tp_at(dx, dl) * WIDE, WIDE), WIDE)
        return matmul_nt(d_kv, wkv[rows, :]).astype(jnp.bfloat16)

    got_di = {}
    for dx in far_first(nx):
        for dl in reversed(range(nl)):
            if (dx, dl) != (0, 0):
                s = dx * nl + dl
                di_snd[s] = term(dx, dl)
                got_di[s] = remote(di_snd.at[s], di_got.at[s], ctx, tp_at(dx, dl))
    d_input = term(0, 0).astype(jnp.float32)

    got_sib[0].wait_recv()
    d_query = dqt[0] * SCALE + dq_sib[0].astype(jnp.float32)
    for dz in near_first(nz):
        got_dq[dz].wait_recv()
        d_query += dq_got[dz].astype(jnp.float32)
    for h in range(GROUP):
        cols = slice(h * HD, (h + 1) * HD)
        dq_res[:, cols] = d_query[:, cols].T.astype(jnp.bfloat16)
    store_dq = local(dq_res, dq_out)

    for s in got_di:
        got_di[s].wait_recv()
        d_input += di_got[s].astype(jnp.float32)
    di_res[...] = d_input.astype(jnp.bfloat16)
    store_di = local(di_res, di_out)
    for copy in sent:
        copy.wait_send()
    store_dq.wait()
    store_di.wait()


def body(grid, x_stash, w_key, w_value, query, out_stash, d_out, roster):
    nz, ny, nx, nl = grid
    nj, nt, chunks = 2 * nz, nx * nl, ny // 2
    bf16, f32 = jnp.bfloat16, jnp.float32
    half = ROPE_BASE ** (-(np.arange(HD // 2) * 2.0) / HD)
    freq = jnp.asarray(np.concatenate([half, half])[None, :].astype(np.float32))
    copies = (nt - 1) + 4 * (nj - 1) + 2 * (ny - 1) + nz + (nz - 1) + (nt - 1)
    vmem = pltpu.VMEM
    hbm = pl.BlockSpec(memory_space=pl.ANY)
    flops = 2 * nj * WIDE * ny * ROWS * HD * 5
    return pl.pallas_call(
        functools.partial(kernel, grid),
        out_shape=(
            jax.ShapeDtypeStruct((ROWS, WIDE), bf16),
            jax.ShapeDtypeStruct((ROWS, WIDE), bf16),
        ),
        in_specs=[hbm] * 6
        + [pl.BlockSpec(memory_space=pltpu.SMEM), pl.BlockSpec(memory_space=pltpu.VMEM)],
        out_specs=(hbm, hbm),
        scratch_shapes=[
            vmem((nt, ROWS, WIDE), bf16),
            vmem((nt * WIDE, 2 * HD), bf16),
            vmem((nj, ROWS, WIDE), bf16),
            vmem((nj, ROWS, WIDE), bf16),
            vmem((ROWS, WIDE), bf16),
            vmem((ny * ROWS, 2 * HD), bf16),
            vmem((chunks, HD, 2 * ROWS), bf16),
            vmem((ny * ROWS, HD), jnp.int32),
            vmem((nj, ROWS), jnp.int32),
            vmem((chunks, nj, 2 * ROWS, WIDE), f32),
            vmem((chunks, nj, 1, WIDE), f32),
            vmem((chunks, nj, 1, WIDE), f32),
            vmem((chunks, nj, 1, WIDE), f32),
            vmem((nj, 1, WIDE), f32),
            vmem((nj, nj, 1, WIDE), f32),
            vmem((nj, 1, WIDE), f32),
            vmem((nj, HD, WIDE), f32),
            vmem((2 * nz, HD, WIDE), bf16),
            vmem((nz, HD, WIDE), bf16),
            vmem((nz, HD, WIDE), bf16),
            vmem((2 * ROWS, 2 * HD), f32),
            vmem((ny, ROWS, 2 * HD), bf16),
            vmem((ny, ROWS, 2 * HD), bf16),
            vmem((nt, ROWS, WIDE), bf16),
            vmem((nt, ROWS, WIDE), bf16),
            vmem((ROWS, WIDE), bf16),
            vmem((ROWS, WIDE), bf16),
            pltpu.SemaphoreType.DMA((copies,)),
            pltpu.SemaphoreType.DMA((copies,)),
            pltpu.SemaphoreType.DMA((8,)),
        ],
        compiler_params=pltpu.CompilerParams(
            collective_id=0, has_side_effects=True, vmem_limit_bytes=56 * 1024 * 1024
        ),
        cost_estimate=pl.CostEstimate(
            flops=flops, bytes_accessed=4 * 1024 * 1024, transcendentals=nj * WIDE * ny * ROWS
        ),
    )(x_stash, w_key, w_value, query, out_stash, d_out, roster, freq)


def solution(mesh):
    grid = GRIDS[mesh.shape["ctx"], mesh.shape["tp"]]
    split = P("ctx", "tp")
    return jax.shard_map(
        functools.partial(body, grid),
        mesh=mesh,
        in_specs=(split, P(None, "tp"), P(None, "tp"), split, split, split, P()),
        out_specs=(split, split),
        check_vma=False,
    )
```

```python
import functools

import jax
import jax.numpy as jnp
import numpy as np
from jax import lax
from jax.experimental import pallas as pl
from jax.experimental.pallas import tpu as pltpu
from jax.sharding import PartitionSpec as P

HD = 128
GROUP = 4
BLOCK = 64
ROWS = 128
WIDE = GROUP * HD
ROPE_BASE = 500000.0
SCALE = HD ** -0.5
LOG2E = 1.4426950408889634
NEG = -1e30
FLOOR = -1e20

GRIDS = {(64, 8): (4, 8, 4, 2)}

NT = (((1,), (1,)), ((), ()))


def matmul_nt(a, b):
    return lax.dot_general(a, b, NT, preferred_element_type=jnp.float32)


def matmul(a, b):
    return jnp.dot(a, b, preferred_element_type=jnp.float32)


def stacked(block):
    return jnp.concatenate([block[:, h * HD:(h + 1) * HD] for h in range(GROUP)], axis=0)


def far_first(count):
    return sorted(range(count), key=lambda d: (-min(d, count - d), d))


def beside(count):
    return sorted({1 % count, count - 1} - {0})


def kernel(
    grid, x_in, wk_in, wv_in, q_in, o_in, g_in, roster, freq,
    dq_out, di_out,
    xg, wkv, qg, gg, ol, kv, kt, posk, posq, probs, peak, total, fac, lse_own, lse_got,
    delta, dqt, dq_snd, dq_sib, dq_half, dq_got, acc, dkv_snd, dkv_got, dkv_all, w_cols, dq_res, di_res,
    send_sem, recv_sem, local_sem,
):
    nz, ny, nx, nl = grid
    nj = 2 * nz
    chunks = ny // 2
    ctx, tp = lax.axis_index("ctx"), lax.axis_index("tp")
    z, y, c = ctx // (2 * ny), (ctx // 2) % ny, ctx % 2
    xi, zl = tp // nl, tp % nl

    def ctx_at(dz, dy, dc):
        return (((z + dz) % nz) * ny + (y + dy) % ny) * 2 + (c + dc) % 2

    def tp_at(dx, dl):
        return ((xi + dx) % nx) * nl + (zl + dl) % nl

    tp_peers = [(dx, dl) for dx in range(nx) for dl in range(nl) if (dx, dl) != (0, 0)]
    q_peers = [(dz, dc) for dz in range(nz) for dc in range(2) if (dz, dc) != (0, 0)]
    y_peers = list(range(1, ny))

    used = [0, 0]

    def local(src, dst):
        copy = pltpu.make_async_copy(src, dst, local_sem.at[used[0]])
        used[0] += 1
        copy.start()
        return copy

    sent = []

    def remote(src, dst, at_ctx, at_tp):
        i = used[1]
        used[1] += 1
        copy = pltpu.make_async_remote_copy(
            src_ref=src, dst_ref=dst, send_sem=send_sem.at[i], recv_sem=recv_sem.at[i],
            device_id=(at_ctx, at_tp), device_id_type=pl.DeviceIdType.MESH,
        )
        copy.start()
        sent.append(copy)
        return copy

    load_x = local(x_in, xg.at[0])
    load_wk = local(wk_in, wkv.at[:, 0:HD])
    load_wv = local(wv_in, wkv.at[:, HD:2 * HD])
    load_g = local(g_in, gg.at[0])
    load_o = local(o_in, ol)
    load_q = local(q_in, qg.at[0])

    barrier = pltpu.get_barrier_semaphore()
    partners = [(ctx, tp_at(dx, dl)) for dx, dl in tp_peers]
    partners += [(ctx_at(dz, 0, dc), tp) for dz, dc in q_peers]
    partners += [(ctx_at(0, dy, 0), tp) for dy in y_peers]
    for partner in partners:
        pl.semaphore_signal(barrier, inc=1, device_id=partner, device_id_type=pl.DeviceIdType.MESH)

    order = far_first(ny)
    place = {dy: p for p, dy in enumerate(order)}
    row_id = lax.broadcasted_iota(jnp.int32, (ROWS, HD), 0)
    lane_id = lax.broadcasted_iota(jnp.int32, (1, ROWS), 1)
    for p, dy in enumerate(order):
        at = ctx_at(0, ny - dy, 0)
        first, second = roster[2 * at] * BLOCK, roster[2 * at + 1] * BLOCK
        posk[p * ROWS:(p + 1) * ROWS, :] = row_id + jnp.where(row_id < BLOCK, first, second - BLOCK)
    for j in range(nj):
        at = ctx_at(nz - j // 2, 0, 2 - j % 2)
        first, second = roster[2 * at] * BLOCK, roster[2 * at + 1] * BLOCK
        posq[j:j + 1, :] = lane_id + jnp.where(lane_id < BLOCK, first, second - BLOCK)
    own = place[0]
    angle = posk[own * ROWS:(own + 1) * ROWS, :].astype(jnp.float32) * freq[...]
    cosine = jnp.cos(angle)
    lane = lax.broadcasted_iota(jnp.int32, (ROWS, HD), 1)
    sine = jnp.where(lane < HD // 2, -1.0, 1.0) * jnp.sin(angle)

    load_g.wait()
    load_o.wait()
    for h in range(GROUP):
        cols = slice(h * HD, (h + 1) * HD)
        product = gg[0, :, cols].astype(jnp.float32) * ol[:, cols].astype(jnp.float32)
        delta[0, :, cols] = jnp.sum(product.T, axis=0, keepdims=True)

    def project(dx, dl):
        at = ((xi + nx - dx) % nx) * nl + (zl + nl - dl) % nl
        rows = pl.ds(pl.multiple_of(at * WIDE, WIDE), WIDE)
        return matmul(xg[dx * nl + dl], wkv[rows, :])

    load_x.wait()
    load_wk.wait()
    load_wv.wait()
    raw = project(0, 0)

    pl.semaphore_wait(barrier, len(partners))

    low, high = slice(0, ROWS // 2), slice(ROWS // 2, ROWS)

    def tp_begin(src, buf):
        got = {}
        if nl > 1:
            got[0, 1] = remote(src, buf.at[1], ctx, tp_at(0, 1))
        for dx in beside(nx):
            got[dx, 0] = remote(src, buf.at[dx * nl], ctx, tp_at(dx, 0))
        return got

    def tp_partner(buf, got):
        if nl > 1:
            got[0, 1].wait_recv()
            for dx in beside(nx):
                got[dx, 1] = remote(buf.at[1], buf.at[dx * nl + 1], ctx, tp_at(dx, 0))

    def tp_sides(buf, got, dl):
        for dx in beside(nx):
            got[dx, dl].wait_recv()
            if nx == 4:
                part = low if dx == 1 else high
                got[2, dl, dx] = remote(
                    buf.at[dx * nl + dl, part, :], buf.at[2 * nl + dl, part, :], ctx, tp_at(dx, 0)
                )

    def tp_opposite(got, dl):
        for dx in beside(nx):
            got[2, dl, dx].wait_recv()

    def z_begin(src, buf):
        got = {}
        for dz in beside(nz):
            got[dz, 0] = remote(src, buf.at[2 * dz], ctx_at(dz, 0, 0), tp)
        got[0, 1] = remote(src, buf.at[1], ctx_at(0, 0, 1), tp)
        return got

    def z_sides(buf, got):
        for dz in beside(nz):
            got[dz, 0].wait_recv()
            if nz == 4:
                part = low if dz == 1 else high
                got[2, 0, dz] = remote(
                    buf.at[2 * dz, part, :], buf.at[4, part, :], ctx_at(dz, 0, 0), tp
                )
            got[dz, 1] = remote(buf.at[2 * dz], buf.at[2 * dz + 1], ctx_at(0, 0, 1), tp)

    def z_opposite(buf, got):
        if nz == 4:
            for dz in beside(nz):
                got[2, 0, dz].wait_recv()
            got[2, 1] = remote(buf.at[4], buf.at[5], ctx_at(0, 0, 1), tp)

    def z_finish(got):
        for dz in range(nz):
            got[dz, 1].wait_recv()

    got_x = tp_begin(x_in, xg)
    got_q = z_begin(q_in, qg)
    tp_partner(xg, got_x)
    tp_sides(xg, got_x, 0)
    if nl > 1:
        raw += project(0, 1)
    for dx in beside(nx):
        raw += project(dx, 0)
    z_sides(qg, got_q)
    got_g = z_begin(g_in, gg)
    got_delta = [
        remote(delta.at[0], delta.at[2 * dz + dc], ctx_at(dz, 0, dc), tp) for dz, dc in q_peers
    ]
    if nl > 1:
        tp_sides(xg, got_x, 1)
        for dx in beside(nx):
            raw += project(dx, 1)
    if nx == 4:
        for dl in range(nl):
            tp_opposite(got_x, dl)
            raw += project(2, dl)

    key_raw = raw[:, 0:HD]
    keys = key_raw * cosine + pltpu.roll(key_raw, HD // 2, 1) * sine
    own_rows = pl.ds(own * ROWS, ROWS)
    kv[own_rows, 0:HD] = keys.astype(jnp.bfloat16)
    kv[own_rows, HD:2 * HD] = raw[:, HD:2 * HD].astype(jnp.bfloat16)

    def kv_send(dy_from, dy_to, start=0, count=ROWS):
        src = kv.at[pl.ds(place[dy_from] * ROWS + start, count), :]
        dst = kv.at[pl.ds(place[dy_to] * ROWS + start, count), :]
        return remote(src, dst, ctx_at(0, (ny + dy_to - dy_from) % ny, 0), tp)

    got_kv = {}
    direct = [1, 7, 2, 6] if ny == 8 else y_peers
    for dy in direct:
        got_kv[dy] = [kv_send(0, dy)]
    z_opposite(qg, got_q)
    if ny == 8:
        got_kv[4] = []
        for dy, onward, start in ((2, 3, 0), (6, 5, ROWS // 2)):
            for copy in got_kv[dy]:
                copy.wait_recv()
            got_kv[dy] = []
            got_kv[onward] = [kv_send(dy, onward)]
            got_kv[4].append(kv_send(dy, 4, start, ROWS // 2))
    load_q.wait()
    z_finish(got_q)
    z_sides(gg, got_g)

    def slot_of(a):
        return ((z + nz - a // 2) % nz) * 2 + (c + 2 - a % 2) % 2

    def place_of(j):
        return ((z + nz - j // 2) % nz) * 2 + (c + 2 - j % 2) % 2

    def score_step(k, a):
        j = slot_of(a)
        rows = pl.ds(pl.multiple_of(k * 2 * ROWS, 2 * ROWS), 2 * ROWS)
        scores = matmul_nt(kv[rows, 0:HD], stacked(qg[j]))
        allowed = posk[rows, :] <= posq[pl.ds(j, 1), :]
        for h in range(GROUP):
            cols = slice(h * HD, (h + 1) * HD)
            part = jnp.where(allowed, scores[:, cols] * (SCALE * LOG2E), NEG)
            top = jnp.maximum(jnp.max(part, axis=0, keepdims=True), FLOOR)
            weight = jnp.exp2(part - top)
            probs[k, j, :, cols] = weight
            peak[k, a, :, cols] = top
            total[k, a, :, cols] = jnp.sum(weight, axis=0, keepdims=True)

    batch = nj // 2

    def send_totals(b):
        for i in range(batch):
            a = b * batch + i
            top = peak[0, a]
            for k in range(1, chunks):
                top = jnp.maximum(top, peak[k, a])
            mass = total[0, a] * jnp.exp2(peak[0, a] - top)
            for k in range(1, chunks):
                mass += total[k, a] * jnp.exp2(peak[k, a] - top)
            lse_own[b, i:i + 1, :] = jnp.where(
                mass > 0.0, top + jnp.log(jnp.maximum(mass, 1e-30)) * LOG2E, NEG
            )
        return [
            remote(lse_own.at[b], lse_got.at[2 * dz + dc, b], ctx_at(dz, 0, dc), tp)
            for dz, dc in q_peers
        ]

    def take_totals(b, got):
        for copy in got:
            copy.wait_recv()
        top = lse_own[b]
        for s in range(1, nj):
            top = jnp.maximum(top, lse_got[s, b])
        mass = jnp.exp2(lse_own[b] - top)
        for s in range(1, nj):
            mass += jnp.exp2(lse_got[s, b] - top)
        lse = top + jnp.log(mass) * LOG2E
        for k in range(chunks):
            for i in range(batch):
                fac[k, b * batch + i] = jnp.exp2(peak[k, b * batch + i] - lse[i:i + 1, :])

    def each(count, step):
        def run(i, carry):
            step(i)
            return carry

        lax.fori_loop(0, count, run, 0)

    for k in reversed(range(chunks)):
        for dy in order[2 * k:2 * k + 2]:
            for copy in got_kv.get(dy, []):
                copy.wait_recv()
        rows = slice(2 * k * ROWS, 2 * (k + 1) * ROWS)
        kt[k] = kv[rows, 0:HD].astype(jnp.float32).T.astype(jnp.bfloat16)
        each(batch, functools.partial(score_step, k))
    got_lse = [send_totals(0)]
    z_opposite(gg, got_g)

    mine = pl.ds(pl.multiple_of(c * HD, HD), HD)
    got_w = {}
    for dx, dl in tp_peers:
        rows = pl.ds(pl.multiple_of(tp_at(dx, dl) * WIDE, WIDE), WIDE)
        s = dx * nl + dl
        got_w[s] = remote(wkv.at[rows, mine], w_cols.at[s, :, mine], ctx, tp_at(dx, dl))

    each(batch * chunks, lambda i: score_step(i // batch, batch + i % batch))
    got_lse.append(send_totals(1))
    for copy in got_delta:
        copy.wait_recv()
    z_finish(got_g)
    take_totals(0, got_lse[0])

    got_dkv = {}
    got_sib = {}
    got_w_sib = {}
    for k in range(chunks):
        rows = slice(2 * k * ROWS, 2 * (k + 1) * ROWS)
        acc[...] = jnp.zeros_like(acc)

        def grad_step(j, k=k, rows=rows):
            gs, qs = stacked(gg[j]), stacked(qg[j])
            d_probs = matmul_nt(kv[rows, HD:2 * HD], gs)
            prob = probs[k, j] * fac[k, place_of(j)]
            d_scores = (prob * (d_probs - delta[j])).astype(jnp.bfloat16)
            acc[:, HD:2 * HD] += matmul(prob.astype(jnp.bfloat16), gs)
            acc[:, 0:HD] += matmul(d_scores, qs)
            part = matmul(kt[k], d_scores)
            if k == 0:
                dqt[j] = part
            else:
                dqt[j] += part

        if k == 0:
            each(batch, lambda a, step=grad_step: step(slot_of(a)))
            take_totals(1, got_lse[1])
            each(batch, lambda a, step=grad_step: step(slot_of(batch + a)))
        if 0 < k < chunks - 1:
            each(nj, grad_step)
        if k == max(chunks - 2, 0):
            for s in got_w:
                got_w[s].wait_recv()
                got_w_sib[s] = remote(
                    w_cols.at[s, :, mine], w_cols.at[s, :, mine], ctx_at(0, 0, 1), tp
                )
        if k == chunks - 1:
            if k:
                each(nz, lambda i, step=grad_step: step(2 * i + 1))
            for dz in far_first(nz):
                dq_snd[dz] = (dqt[2 * dz + 1] * SCALE).astype(jnp.bfloat16)
                got_sib[dz] = remote(dq_snd.at[dz], dq_sib.at[dz], ctx_at(0, 0, 1), tp)
            if k:
                each(nz, lambda i, step=grad_step: step(2 * i))
        for i, dy in enumerate(order[2 * k:2 * k + 2]):
            if dy == 0:
                continue
            p = 2 * k + i
            part = acc[i * ROWS:(i + 1) * ROWS, :]
            dkv_snd[p, :, 0:HD] = (part[:, 0:HD] * SCALE).astype(jnp.bfloat16)
            dkv_snd[p, :, HD:2 * HD] = part[:, HD:2 * HD].astype(jnp.bfloat16)
            got_dkv[dy] = remote(dkv_snd.at[p], dkv_got.at[p], ctx_at(0, ny - dy, 0), tp)

    def both_cores(dz):
        got_sib[dz].wait_recv()
        return dqt[2 * dz] * SCALE + dq_sib[dz].astype(jnp.float32)

    got_half = {}
    if nz == 4:
        dq_snd[6] = both_cores(2).astype(jnp.bfloat16)
        got_half[1] = remote(dq_snd.at[6, low, :], dq_half.at[low, :], ctx_at(3, 0, 0), tp)
        got_half[3] = remote(dq_snd.at[6, high, :], dq_half.at[high, :], ctx_at(1, 0, 0), tp)

    i = own % 2
    d_key = acc[i * ROWS:(i + 1) * ROWS, 0:HD] * SCALE
    d_value = acc[i * ROWS:(i + 1) * ROWS, HD:2 * HD]
    for dy in order:
        if dy:
            got_dkv[dy].wait_recv()
            d_key += dkv_got[place[dy], :, 0:HD].astype(jnp.float32)
            d_value += dkv_got[place[dy], :, HD:2 * HD].astype(jnp.float32)
    d_key = d_key * cosine - pltpu.roll(d_key, HD // 2, 1) * sine
    d_kv = jnp.concatenate([d_key, d_value], axis=1).astype(jnp.bfloat16)
    dkv_all[0] = d_kv
    got_all = tp_begin(dkv_all.at[0], dkv_all)

    got_dq = {}
    for dz in beside(nz):
        both = both_cores(dz)
        if nz == 4:
            got_half[dz].wait_recv()
            part = low if dz == 1 else high
            other = high if dz == 1 else low
            dq_snd[nz + dz, part, :] = (
                both[part] + dq_half[part, :].astype(jnp.float32)
            ).astype(jnp.bfloat16)
            dq_snd[nz + dz, other, :] = both[other].astype(jnp.bfloat16)
        else:
            dq_snd[nz + dz] = both.astype(jnp.bfloat16)
        got_dq[dz] = remote(dq_snd.at[nz + dz], dq_got.at[dz], ctx_at(nz - dz, 0, 0), tp)
    tp_partner(dkv_all, got_all)
    tp_sides(dkv_all, got_all, 0)

    def term(s, weights):
        return matmul_nt(dkv_all[s], weights).astype(jnp.bfloat16).astype(jnp.float32)

    for s in got_w_sib:
        got_w_sib[s].wait_recv()
    d_input = term(0, wkv[pl.ds(pl.multiple_of(tp * WIDE, WIDE), WIDE), :])
    if nl > 1:
        d_input += term(1, w_cols[1])
    for dx in beside(nx):
        d_input += term(dx * nl, w_cols[dx * nl])
    if nl > 1:
        tp_sides(dkv_all, got_all, 1)
        for dx in beside(nx):
            d_input += term(dx * nl + 1, w_cols[dx * nl + 1])
    if nx == 4:
        for dl in range(nl):
            tp_opposite(got_all, dl)
            d_input += term(2 * nl + dl, w_cols[2 * nl + dl])
    di_res[...] = d_input.astype(jnp.bfloat16)
    store_di = local(di_res, di_out)

    d_query = both_cores(0)
    for dz in beside(nz):
        got_dq[dz].wait_recv()
        d_query += dq_got[dz].astype(jnp.float32)
    for h in range(GROUP):
        cols = slice(h * HD, (h + 1) * HD)
        dq_res[:, cols] = d_query[:, cols].T.astype(jnp.bfloat16)
    store_dq = local(dq_res, dq_out)
    for copy in sent:
        copy.wait_send()
    store_dq.wait()
    store_di.wait()


def body(grid, x_stash, w_key, w_value, query, out_stash, d_out, roster):
    nz, ny, nx, nl = grid
    nj, nt, chunks = 2 * nz, nx * nl, ny // 2
    bf16, f32 = jnp.bfloat16, jnp.float32
    half = ROPE_BASE ** (-(np.arange(HD // 2) * 2.0) / HD)
    freq = jnp.asarray(np.concatenate([half, half])[None, :].astype(np.float32))
    copies = 128
    vmem = pltpu.VMEM
    hbm = pl.BlockSpec(memory_space=pl.ANY)
    flops = 2 * nj * WIDE * ny * ROWS * HD * 5
    return pl.pallas_call(
        functools.partial(kernel, grid),
        out_shape=(
            jax.ShapeDtypeStruct((ROWS, WIDE), bf16),
            jax.ShapeDtypeStruct((ROWS, WIDE), bf16),
        ),
        in_specs=[hbm] * 6
        + [pl.BlockSpec(memory_space=pltpu.SMEM), pl.BlockSpec(memory_space=pltpu.VMEM)],
        out_specs=(hbm, hbm),
        scratch_shapes=[
            vmem((nt, ROWS, WIDE), bf16),
            vmem((nt * WIDE, 2 * HD), bf16),
            vmem((nj, ROWS, WIDE), bf16),
            vmem((nj, ROWS, WIDE), bf16),
            vmem((ROWS, WIDE), bf16),
            vmem((ny * ROWS, 2 * HD), bf16),
            vmem((chunks, HD, 2 * ROWS), bf16),
            vmem((ny * ROWS, HD), jnp.int32),
            vmem((nj, ROWS), jnp.int32),
            vmem((chunks, nj, 2 * ROWS, WIDE), f32),
            vmem((chunks, nj, 1, WIDE), f32),
            vmem((chunks, nj, 1, WIDE), f32),
            vmem((chunks, nj, 1, WIDE), f32),
            vmem((2, nz, WIDE), f32),
            vmem((nj, 2, nz, WIDE), f32),
            vmem((nj, 1, WIDE), f32),
            vmem((nj, HD, WIDE), f32),
            vmem((2 * nz, HD, WIDE), bf16),
            vmem((nz, HD, WIDE), bf16),
            vmem((HD, WIDE), bf16),
            vmem((nz, HD, WIDE), bf16),
            vmem((2 * ROWS, 2 * HD), f32),
            vmem((ny, ROWS, 2 * HD), bf16),
            vmem((ny, ROWS, 2 * HD), bf16),
            vmem((nt, ROWS, 2 * HD), bf16),
            vmem((nt, WIDE, 2 * HD), bf16),
            vmem((ROWS, WIDE), bf16),
            vmem((ROWS, WIDE), bf16),
            pltpu.SemaphoreType.DMA((copies,)),
            pltpu.SemaphoreType.DMA((copies,)),
            pltpu.SemaphoreType.DMA((8,)),
        ],
        compiler_params=pltpu.CompilerParams(
            collective_id=0, has_side_effects=True, vmem_limit_bytes=56 * 1024 * 1024
        ),
        cost_estimate=pl.CostEstimate(
            flops=flops, bytes_accessed=4 * 1024 * 1024, transcendentals=nj * WIDE * ny * ROWS
        ),
    )(x_stash, w_key, w_value, query, out_stash, d_out, roster, freq)


def solution(mesh):
    grid = GRIDS[mesh.shape["ctx"], mesh.shape["tp"]]
    split = P("ctx", "tp")
    return jax.shard_map(
        functools.partial(body, grid),
        mesh=mesh,
        in_specs=(split, P(None, "tp"), P(None, "tp"), split, split, split, P()),
        out_specs=(split, split),
        check_vma=False,
    )
```

```python
import functools

import jax
import jax.numpy as jnp
import numpy as np
from jax import lax
from jax.experimental import pallas as pl
from jax.experimental.pallas import tpu as pltpu
from jax.sharding import PartitionSpec as P

HD = 128
GROUP = 4
BLOCK = 64
ROWS = 128
WIDE = GROUP * HD
ROPE_BASE = 500000.0
SCALE = HD ** -0.5
LOG2E = 1.4426950408889634
NEG = -1e30
FLOOR = -1e20

GRIDS = {(64, 8): (4, 8, 4, 2)}

NT = (((1,), (1,)), ((), ()))


def matmul_nt(a, b):
    return lax.dot_general(a, b, NT, preferred_element_type=jnp.float32)


def matmul(a, b):
    return jnp.dot(a, b, preferred_element_type=jnp.float32)


def stacked(block):
    return jnp.concatenate([block[:, h * HD:(h + 1) * HD] for h in range(GROUP)], axis=0)


def far_first(count):
    return sorted(range(count), key=lambda d: (-min(d, count - d), d))


def key_order(ny):
    return [4, 3, 5, 7, 2, 6, 1, 0] if ny == 8 else far_first(ny)


def beside(count):
    return sorted({1 % count, count - 1} - {0})


def kernel(
    grid, x_in, wk_in, wv_in, q_in, o_in, g_in, roster, freq,
    dq_out, di_out,
    xg, wkv, qg, gg, ol, kv, kt, posk, posq, probs, peak, total, fac, lse_own, lse_got,
    delta, dqt, dq_snd, dq_sib, dq_half, dq_got, acc, dkv_snd, dkv_relay, dkv_got, dkv_all, w_cols, dq_res, di_res,
    send_sem, recv_sem, local_sem,
):
    nz, ny, nx, nl = grid
    nj = 2 * nz
    chunks = ny // 2
    ctx, tp = lax.axis_index("ctx"), lax.axis_index("tp")
    z, y, c = ctx // (2 * ny), (ctx // 2) % ny, ctx % 2
    xi, zl = tp // nl, tp % nl

    def ctx_at(dz, dy, dc):
        return (((z + dz) % nz) * ny + (y + dy) % ny) * 2 + (c + dc) % 2

    def tp_at(dx, dl):
        return ((xi + dx) % nx) * nl + (zl + dl) % nl

    tp_peers = [(dx, dl) for dx in range(nx) for dl in range(nl) if (dx, dl) != (0, 0)]
    q_peers = [(dz, dc) for dz in range(nz) for dc in range(2) if (dz, dc) != (0, 0)]
    y_peers = list(range(1, ny))

    used = [0, 0]

    def local(src, dst):
        copy = pltpu.make_async_copy(src, dst, local_sem.at[used[0]])
        used[0] += 1
        copy.start()
        return copy

    sent = []

    def remote(src, dst, at_ctx, at_tp):
        i = used[1]
        used[1] += 1
        copy = pltpu.make_async_remote_copy(
            src_ref=src, dst_ref=dst, send_sem=send_sem.at[i], recv_sem=recv_sem.at[i],
            device_id=(at_ctx, at_tp), device_id_type=pl.DeviceIdType.MESH,
        )
        copy.start()
        sent.append(copy)
        return copy

    load_x = local(x_in, xg.at[0])
    load_wk = local(wk_in, wkv.at[:, 0:HD])
    load_wv = local(wv_in, wkv.at[:, HD:2 * HD])
    load_g = local(g_in, gg.at[0])
    load_o = local(o_in, ol)
    load_q = local(q_in, qg.at[0])

    barrier = pltpu.get_barrier_semaphore()
    partners = [(ctx, tp_at(dx, dl)) for dx, dl in tp_peers]
    partners += [(ctx_at(dz, 0, dc), tp) for dz, dc in q_peers]
    partners += [(ctx_at(0, dy, 0), tp) for dy in y_peers]
    for partner in partners:
        pl.semaphore_signal(barrier, inc=1, device_id=partner, device_id_type=pl.DeviceIdType.MESH)

    order = key_order(ny)
    place = {dy: p for p, dy in enumerate(order)}
    row_id = lax.broadcasted_iota(jnp.int32, (ROWS, HD), 0)
    lane_id = lax.broadcasted_iota(jnp.int32, (1, ROWS), 1)
    for p, dy in enumerate(order):
        at = ctx_at(0, ny - dy, 0)
        first, second = roster[2 * at] * BLOCK, roster[2 * at + 1] * BLOCK
        posk[p * ROWS:(p + 1) * ROWS, :] = row_id + jnp.where(row_id < BLOCK, first, second - BLOCK)
    for j in range(nj):
        at = ctx_at(nz - j // 2, 0, 2 - j % 2)
        first, second = roster[2 * at] * BLOCK, roster[2 * at + 1] * BLOCK
        posq[j:j + 1, :] = lane_id + jnp.where(lane_id < BLOCK, first, second - BLOCK)
    own = place[0]
    angle = posk[own * ROWS:(own + 1) * ROWS, :].astype(jnp.float32) * freq[...]
    cosine = jnp.cos(angle)
    lane = lax.broadcasted_iota(jnp.int32, (ROWS, HD), 1)
    sine = jnp.where(lane < HD // 2, -1.0, 1.0) * jnp.sin(angle)

    load_g.wait()
    load_o.wait()
    for h in range(GROUP):
        cols = slice(h * HD, (h + 1) * HD)
        product = gg[0, :, cols].astype(jnp.float32) * ol[:, cols].astype(jnp.float32)
        delta[0, :, cols] = jnp.sum(product.T, axis=0, keepdims=True)

    def project(dx, dl):
        at = ((xi + nx - dx) % nx) * nl + (zl + nl - dl) % nl
        rows = pl.ds(pl.multiple_of(at * WIDE, WIDE), WIDE)
        return matmul(xg[dx * nl + dl], wkv[rows, :])

    load_x.wait()
    load_wk.wait()
    load_wv.wait()
    raw = project(0, 0)

    pl.semaphore_wait(barrier, len(partners))

    low, high = slice(0, ROWS // 2), slice(ROWS // 2, ROWS)

    def tp_begin(src, buf, across=False):
        got = {}
        if nl > 1:
            got[0, 1] = remote(src, buf.at[1], ctx, tp_at(0, 1))
        for dl in range(nl if across else 1):
            for dx in beside(nx):
                got[dx, dl] = remote(src, buf.at[dx * nl + dl], ctx, tp_at(dx, dl))
        return got

    def tp_partner(buf, got):
        if nl > 1:
            got[0, 1].wait_recv()
            for dx in beside(nx):
                got[dx, 1] = remote(buf.at[1], buf.at[dx * nl + 1], ctx, tp_at(dx, 0))

    def tp_sides(buf, got, dl):
        for dx in beside(nx):
            got[dx, dl].wait_recv()
            if nx == 4:
                part = low if dx == 1 else high
                got[2, dl, dx] = remote(
                    buf.at[dx * nl + dl, part, :], buf.at[2 * nl + dl, part, :], ctx, tp_at(dx, 0)
                )

    def tp_opposite(got, dl):
        for dx in beside(nx):
            got[2, dl, dx].wait_recv()

    def z_begin(src, buf):
        got = {}
        for dz in beside(nz):
            got[dz, 0] = remote(src, buf.at[2 * dz], ctx_at(dz, 0, 0), tp)
        got[0, 1] = remote(src, buf.at[1], ctx_at(0, 0, 1), tp)
        return got

    def z_sides(buf, got):
        for dz in beside(nz):
            got[dz, 0].wait_recv()
            if nz == 4:
                part = low if dz == 1 else high
                got[2, 0, dz] = remote(
                    buf.at[2 * dz, part, :], buf.at[4, part, :], ctx_at(dz, 0, 0), tp
                )
            got[dz, 1] = remote(buf.at[2 * dz], buf.at[2 * dz + 1], ctx_at(0, 0, 1), tp)

    def z_opposite(buf, got):
        if nz == 4:
            for dz in beside(nz):
                got[2, 0, dz].wait_recv()
            got[2, 1] = remote(buf.at[4], buf.at[5], ctx_at(0, 0, 1), tp)

    def z_finish(got):
        for dz in range(nz):
            got[dz, 1].wait_recv()

    got_x = tp_begin(x_in, xg)
    tp_partner(xg, got_x)
    got_q = z_begin(q_in, qg)
    tp_sides(xg, got_x, 0)
    if nl > 1:
        raw += project(0, 1)
    for dx in beside(nx):
        raw += project(dx, 0)
    if nl > 1:
        tp_sides(xg, got_x, 1)
    z_sides(qg, got_q)
    if nl > 1:
        for dx in beside(nx):
            raw += project(dx, 1)
    if nx == 4:
        for dl in range(nl):
            tp_opposite(got_x, dl)
            raw += project(2, dl)

    key_raw = raw[:, 0:HD]
    keys = key_raw * cosine + pltpu.roll(key_raw, HD // 2, 1) * sine
    own_rows = pl.ds(own * ROWS, ROWS)
    kv[own_rows, 0:HD] = keys.astype(jnp.bfloat16)
    kv[own_rows, HD:2 * HD] = raw[:, HD:2 * HD].astype(jnp.bfloat16)

    def kv_send(dy_from, dy_to, start=0, count=ROWS):
        src = kv.at[pl.ds(place[dy_from] * ROWS + start, count), :]
        dst = kv.at[pl.ds(place[dy_to] * ROWS + start, count), :]
        return remote(src, dst, ctx_at(0, (ny + dy_to - dy_from) % ny, 0), tp)

    got_kv = {}
    direct = [1, 7, 2, 6] if ny == 8 else y_peers
    for dy in direct:
        got_kv[dy] = [kv_send(0, dy)]
    got_g = z_begin(g_in, gg)
    got_delta = [
        remote(delta.at[0], delta.at[2 * dz + dc], ctx_at(dz, 0, dc), tp) for dz, dc in q_peers
    ]
    z_opposite(qg, got_q)
    load_q.wait()

    def kv_forward():
        if ny == 8:
            got_kv[4] = []
            for dy, onward, start in ((2, 3, 0), (6, 5, ROWS // 2)):
                for copy in got_kv[dy]:
                    copy.wait_recv()
                got_kv[dy] = []
                got_kv[onward] = [kv_send(dy, onward)]
                got_kv[4].append(kv_send(dy, 4, start, ROWS // 2))

    def slot_of(a):
        return ((z + nz - a // 2) % nz) * 2 + (c + 2 - a % 2) % 2

    def place_of(j):
        return ((z + nz - j // 2) % nz) * 2 + (c + 2 - j % 2) % 2

    def score_step(k, a):
        j = slot_of(a)
        rows = pl.ds(pl.multiple_of(k * 2 * ROWS, 2 * ROWS), 2 * ROWS)
        scores = matmul_nt(kv[rows, 0:HD], stacked(qg[j]))
        allowed = posk[rows, :] <= posq[pl.ds(j, 1), :]
        for h in range(GROUP):
            cols = slice(h * HD, (h + 1) * HD)
            part = jnp.where(allowed, scores[:, cols] * (SCALE * LOG2E), NEG)
            top = jnp.maximum(jnp.max(part, axis=0, keepdims=True), FLOOR)
            weight = jnp.exp2(part - top)
            probs[k, j, :, cols] = weight
            peak[k, a, :, cols] = top
            total[k, a, :, cols] = jnp.sum(weight, axis=0, keepdims=True)

    batch = nj // 2

    def send_totals(b):
        for i in range(batch):
            a = b * batch + i
            top = peak[0, a]
            for k in range(1, chunks):
                top = jnp.maximum(top, peak[k, a])
            mass = total[0, a] * jnp.exp2(peak[0, a] - top)
            for k in range(1, chunks):
                mass += total[k, a] * jnp.exp2(peak[k, a] - top)
            lse_own[b, i:i + 1, :] = jnp.where(
                mass > 0.0, top + jnp.log(jnp.maximum(mass, 1e-30)) * LOG2E, NEG
            )
        return [
            remote(lse_own.at[b], lse_got.at[2 * dz + dc, b], ctx_at(dz, 0, dc), tp)
            for dz, dc in q_peers
        ]

    def take_totals(b, got):
        for copy in got:
            copy.wait_recv()
        top = lse_own[b]
        for s in range(1, nj):
            top = jnp.maximum(top, lse_got[s, b])
        mass = jnp.exp2(lse_own[b] - top)
        for s in range(1, nj):
            mass += jnp.exp2(lse_got[s, b] - top)
        lse = top + jnp.log(mass) * LOG2E
        for k in range(chunks):
            for i in range(batch):
                fac[k, b * batch + i] = jnp.exp2(peak[k, b * batch + i] - lse[i:i + 1, :])

    def each(count, step):
        unit = 4 if count % 4 == 0 else 1

        def run(i, carry):
            for u in range(unit):
                step(i * unit + u)
            return carry

        lax.fori_loop(0, count // unit, run, 0)

    mine = pl.ds(pl.multiple_of(c * HD, HD), HD)
    got_w = {}

    def send_weights(peers):
        for dx, dl in peers:
            rows = pl.ds(pl.multiple_of(tp_at(dx, dl) * WIDE, WIDE), WIDE)
            s = dx * nl + dl
            got_w[s] = remote(wkv.at[rows, mine], w_cols.at[s, :, mine], ctx, tp_at(dx, dl))

    got_w_sib = {}

    def share_weights(slots):
        for s in slots:
            if s not in got_w_sib:
                got_w[s].wait_recv()
                got_w_sib[s] = remote(
                    w_cols.at[s, :, mine], w_cols.at[s, :, mine], ctx_at(0, 0, 1), tp
                )

    z_finish(got_q)
    for k in reversed(range(chunks)):
        for dy in order[2 * k:2 * k + 2]:
            for copy in got_kv.get(dy, []):
                copy.wait_recv()
        rows = slice(2 * k * ROWS, 2 * (k + 1) * ROWS)
        kt[k] = kv[rows, 0:HD].astype(jnp.float32).T.astype(jnp.bfloat16)
        if k:
            each(nj, functools.partial(score_step, k))
        if k == chunks - 1:
            kv_forward()
            send_weights([(dx, dl) for dx, dl in tp_peers if dl == 0])
        if k == max(chunks - 2, 0):
            z_sides(gg, got_g)
    got_lse = []
    for b in range(2):
        each(batch, lambda i, first=b * batch: score_step(0, first + i))
        got_lse.append(send_totals(b))
    z_opposite(gg, got_g)
    for copy in got_delta:
        copy.wait_recv()
    z_finish(got_g)
    take_totals(0, got_lse[0])

    got_dkv = {}
    got_sib = {}
    got_relay = {}

    def dkv_send(dy, to, dst, start=0, count=ROWS):
        src = dkv_snd.at[place[dy], pl.ds(start, count), :]
        return remote(src, dst.at[pl.ds(start, count), :], ctx_at(0, (ny + to) % ny, 0), tp)

    for k in range(chunks):
        rows = slice(2 * k * ROWS, 2 * (k + 1) * ROWS)
        acc[...] = jnp.zeros_like(acc)

        def grad_step(j, k=k, rows=rows):
            gs, qs = stacked(gg[j]), stacked(qg[j])
            d_probs = matmul_nt(kv[rows, HD:2 * HD], gs)
            prob = probs[k, j] * fac[k, place_of(j)]
            d_scores = (prob * (d_probs - delta[j])).astype(jnp.bfloat16)
            acc[:, HD:2 * HD] += matmul(prob.astype(jnp.bfloat16), gs)
            acc[:, 0:HD] += matmul(d_scores, qs)
            part = matmul(kt[k], d_scores)
            if k == 0:
                dqt[j] = part
            else:
                dqt[j] += part

        if k == 0:
            each(batch, lambda a, step=grad_step: step(slot_of(a)))
            take_totals(1, got_lse[1])
            send_weights([(dx, dl) for dx, dl in tp_peers if dl])
            each(batch, lambda a, step=grad_step: step(slot_of(batch + a)))
        if 0 < k < chunks - 1:
            each(nj, grad_step)
        if k == chunks - 1:
            if k:
                each(nz, lambda i, step=grad_step: step(2 * i + 1))
            for dz in far_first(nz):
                dq_snd[dz] = (dqt[2 * dz + 1] * SCALE).astype(jnp.bfloat16)
                got_sib[dz] = remote(dq_snd.at[dz], dq_sib.at[dz], ctx_at(0, 0, 1), tp)
            if k:
                each(nz, lambda i, step=grad_step: step(2 * i))
        for i, dy in enumerate(order[2 * k:2 * k + 2]):
            if dy == 0:
                continue
            p = 2 * k + i
            part = acc[i * ROWS:(i + 1) * ROWS, :]
            d_key, d_value = part[:, 0:HD] * SCALE, part[:, HD:2 * HD]
            if ny == 8 and dy in (2, 6):
                side, half = (0, low) if dy == 2 else (1, high)
                got_relay[dy].wait_recv()
                got_relay[4, dy].wait_recv()
                d_key += dkv_relay[side, :, 0:HD].astype(jnp.float32)
                d_value += dkv_relay[side, :, HD:2 * HD].astype(jnp.float32)
                more = dkv_relay[2, half, :].astype(jnp.float32)
                none = jnp.zeros_like(more)
                more = jnp.concatenate([more, none] if dy == 2 else [none, more], axis=0)
                d_key += more[:, 0:HD]
                d_value += more[:, HD:2 * HD]
            dkv_snd[p, :, 0:HD] = d_key.astype(jnp.bfloat16)
            dkv_snd[p, :, HD:2 * HD] = d_value.astype(jnp.bfloat16)
            if ny == 8 and dy == 4:
                got_relay[4, 2] = dkv_send(4, -2, dkv_relay.at[2], 0, ROWS // 2)
                got_relay[4, 6] = dkv_send(4, 2, dkv_relay.at[2], ROWS // 2, ROWS // 2)
            elif ny == 8 and dy in (3, 5):
                side = 0 if dy == 3 else 1
                got_relay[2 if dy == 3 else 6] = dkv_send(dy, -1 if dy == 3 else 1, dkv_relay.at[side])
            else:
                got_dkv[dy] = dkv_send(dy, -dy, dkv_got.at[p])
        if k == min(1, chunks - 1):
            share_weights([dx * nl for dx, dl in tp_peers if dl == 0])

    def both_cores(dz):
        got_sib[dz].wait_recv()
        return dqt[2 * dz] * SCALE + dq_sib[dz].astype(jnp.float32)

    got_half = {}
    if nz == 4:
        dq_snd[2 * nz - 2] = both_cores(2).astype(jnp.bfloat16)
        got_half[1] = remote(dq_snd.at[2 * nz - 2, low, :], dq_half.at[low, :], ctx_at(3, 0, 0), tp)
        got_half[3] = remote(dq_snd.at[2 * nz - 2, high, :], dq_half.at[high, :], ctx_at(1, 0, 0), tp)

    i = own % 2
    d_key = acc[i * ROWS:(i + 1) * ROWS, 0:HD] * SCALE
    d_value = acc[i * ROWS:(i + 1) * ROWS, HD:2 * HD]
    for dy in got_dkv:
        got_dkv[dy].wait_recv()
        d_key += dkv_got[place[dy], :, 0:HD].astype(jnp.float32)
        d_value += dkv_got[place[dy], :, HD:2 * HD].astype(jnp.float32)
    d_key = d_key * cosine - pltpu.roll(d_key, HD // 2, 1) * sine
    d_kv = jnp.concatenate([d_key, d_value], axis=1).astype(jnp.bfloat16)
    dkv_all[0] = d_kv
    got_all = tp_begin(dkv_all.at[0], dkv_all, across=True)
    share_weights([dx * nl + dl for dx, dl in tp_peers if dl])

    got_dq = {}
    for dz in beside(nz):
        both = both_cores(dz)
        if nz == 4:
            got_half[dz].wait_recv()
            part = low if dz == 1 else high
            other = high if dz == 1 else low
            dq_snd[nz + dz, part, :] = (
                both[part] + dq_half[part, :].astype(jnp.float32)
            ).astype(jnp.bfloat16)
            dq_snd[nz + dz, other, :] = both[other].astype(jnp.bfloat16)
        else:
            dq_snd[nz + dz] = both.astype(jnp.bfloat16)
        got_dq[dz] = remote(dq_snd.at[nz + dz], dq_got.at[dz], ctx_at(nz - dz, 0, 0), tp)
    for dl in range(nl):
        tp_sides(dkv_all, got_all, dl)
    if nl > 1:
        got_all[0, 1].wait_recv()

    def term(s, weights):
        return matmul_nt(dkv_all[s], weights).astype(jnp.bfloat16).astype(jnp.float32)

    for s in got_w_sib:
        got_w_sib[s].wait_recv()
    d_input = term(0, wkv[pl.ds(pl.multiple_of(tp * WIDE, WIDE), WIDE), :])
    if nl > 1:
        d_input += term(1, w_cols[1])
    for dx in beside(nx):
        d_input += term(dx * nl, w_cols[dx * nl])
    if nl > 1:
        for dx in beside(nx):
            d_input += term(dx * nl + 1, w_cols[dx * nl + 1])
    if nx == 4:
        for dl in range(nl):
            tp_opposite(got_all, dl)
            d_input += term(2 * nl + dl, w_cols[2 * nl + dl])
    di_res[...] = d_input.astype(jnp.bfloat16)
    store_di = local(di_res, di_out)

    d_query = both_cores(0)
    for dz in beside(nz):
        got_dq[dz].wait_recv()
        d_query += dq_got[dz].astype(jnp.float32)
    for h in range(GROUP):
        cols = slice(h * HD, (h + 1) * HD)
        dq_res[:, cols] = d_query[:, cols].T.astype(jnp.bfloat16)
    store_dq = local(dq_res, dq_out)
    for copy in sent:
        copy.wait_send()
    store_dq.wait()
    store_di.wait()


def body(grid, x_stash, w_key, w_value, query, out_stash, d_out, roster):
    nz, ny, nx, nl = grid
    nj, nt, chunks = 2 * nz, nx * nl, ny // 2
    bf16, f32 = jnp.bfloat16, jnp.float32
    half = ROPE_BASE ** (-(np.arange(HD // 2) * 2.0) / HD)
    freq = jnp.asarray(np.concatenate([half, half])[None, :].astype(np.float32))
    copies = 128
    vmem = pltpu.VMEM
    hbm = pl.BlockSpec(memory_space=pl.ANY)
    flops = 2 * nj * WIDE * ny * ROWS * HD * 5
    return pl.pallas_call(
        functools.partial(kernel, grid),
        out_shape=(
            jax.ShapeDtypeStruct((ROWS, WIDE), bf16),
            jax.ShapeDtypeStruct((ROWS, WIDE), bf16),
        ),
        in_specs=[hbm] * 6
        + [pl.BlockSpec(memory_space=pltpu.SMEM), pl.BlockSpec(memory_space=pltpu.VMEM)],
        out_specs=(hbm, hbm),
        scratch_shapes=[
            vmem((nt, ROWS, WIDE), bf16),
            vmem((nt * WIDE, 2 * HD), bf16),
            vmem((nj, ROWS, WIDE), bf16),
            vmem((nj, ROWS, WIDE), bf16),
            vmem((ROWS, WIDE), bf16),
            vmem((ny * ROWS, 2 * HD), bf16),
            vmem((chunks, HD, 2 * ROWS), bf16),
            vmem((ny * ROWS, HD), jnp.int32),
            vmem((nj, ROWS), jnp.int32),
            vmem((chunks, nj, 2 * ROWS, WIDE), f32),
            vmem((chunks, nj, 1, WIDE), f32),
            vmem((chunks, nj, 1, WIDE), f32),
            vmem((chunks, nj, 1, WIDE), f32),
            vmem((2, nz, WIDE), f32),
            vmem((nj, 2, nz, WIDE), f32),
            vmem((nj, 1, WIDE), f32),
            vmem((nj, HD, WIDE), f32),
            vmem((2 * nz, HD, WIDE), bf16),
            vmem((nz, HD, WIDE), bf16),
            vmem((HD, WIDE), bf16),
            vmem((nz, HD, WIDE), bf16),
            vmem((2 * ROWS, 2 * HD), f32),
            vmem((ny, ROWS, 2 * HD), bf16),
            vmem((3, ROWS, 2 * HD), bf16),
            vmem((ny, ROWS, 2 * HD), bf16),
            vmem((nt, ROWS, 2 * HD), bf16),
            vmem((nt, WIDE, 2 * HD), bf16),
            vmem((ROWS, WIDE), bf16),
            vmem((ROWS, WIDE), bf16),
            pltpu.SemaphoreType.DMA((copies,)),
            pltpu.SemaphoreType.DMA((copies,)),
            pltpu.SemaphoreType.DMA((8,)),
        ],
        compiler_params=pltpu.CompilerParams(
            collective_id=0, has_side_effects=True, vmem_limit_bytes=56 * 1024 * 1024
        ),
        cost_estimate=pl.CostEstimate(
            flops=flops, bytes_accessed=4 * 1024 * 1024, transcendentals=nj * WIDE * ny * ROWS
        ),
    )(x_stash, w_key, w_value, query, out_stash, d_out, roster, freq)


def solution(mesh):
    grid = GRIDS[mesh.shape["ctx"], mesh.shape["tp"]]
    split = P("ctx", "tp")
    return jax.shard_map(
        functools.partial(body, grid),
        mesh=mesh,
        in_specs=(split, P(None, "tp"), P(None, "tp"), split, split, split, P()),
        out_specs=(split, split),
        check_vma=False,
    )
```

```python
import functools

import jax
import jax.numpy as jnp
import numpy as np
from jax import lax
from jax.experimental import pallas as pl
from jax.experimental.pallas import tpu as pltpu
from jax.sharding import PartitionSpec as P

HD = 128
GROUP = 4
BLOCK = 64
ROWS = 128
WIDE = GROUP * HD
ROPE_BASE = 500000.0
SCALE = HD ** -0.5
LOG2E = 1.4426950408889634
NEG = -1e30
FLOOR = -1e20

GRIDS = {(64, 8): (4, 8, 4, 2)}

NT = (((1,), (1,)), ((), ()))


def matmul_nt(a, b):
    return lax.dot_general(a, b, NT, preferred_element_type=jnp.float32)


def matmul(a, b):
    return jnp.dot(a, b, preferred_element_type=jnp.float32)


def stacked(block):
    return jnp.concatenate([block[:, h * HD:(h + 1) * HD] for h in range(GROUP)], axis=0)


def far_first(count):
    return sorted(range(count), key=lambda d: (-min(d, count - d), d))


def key_order(ny):
    return [4, 3, 5, 7, 2, 6, 1, 0] if ny == 8 else far_first(ny)


def beside(count):
    return sorted({1 % count, count - 1} - {0})


def kernel(
    grid, x_in, wk_in, wv_in, q_in, o_in, g_in, roster, freq,
    dq_out, di_out,
    xg, wkv, qg, gg, ol, kv, kt, posk, posq, probs, peak, total, fac, lse_own, lse_got,
    delta, ahead, dqt, dq_snd, dq_sib, dq_half, dq_got, acc, dkv_snd, dkv_relay, dkv_got, dkv_all, w_cols, di_snd, di_got, dq_res, di_res,
    send_sem, recv_sem, local_sem,
):
    nz, ny, nx, nl = grid
    nj = 2 * nz
    chunks = ny // 2
    ctx, tp = lax.axis_index("ctx"), lax.axis_index("tp")
    z, y, c = ctx // (2 * ny), (ctx // 2) % ny, ctx % 2
    xi, zl = tp // nl, tp % nl

    def ctx_at(dz, dy, dc):
        return (((z + dz) % nz) * ny + (y + dy) % ny) * 2 + (c + dc) % 2

    def tp_at(dx, dl):
        return ((xi + dx) % nx) * nl + (zl + dl) % nl

    tp_peers = [(dx, 0) for dx in range(1, nx)] + [(0, dl) for dl in range(1, nl)]
    q_peers = [(dz, dc) for dz in range(nz) for dc in range(2) if (dz, dc) != (0, 0)]
    direct = [1, 7, 2, 6] if ny == 8 else list(range(1, ny))

    used = [0, 0]

    def local(src, dst):
        copy = pltpu.make_async_copy(src, dst, local_sem.at[used[0]])
        used[0] += 1
        copy.start()
        return copy

    sent = []

    def remote(src, dst, at_ctx, at_tp):
        i = used[1]
        used[1] += 1
        copy = pltpu.make_async_remote_copy(
            src_ref=src, dst_ref=dst, send_sem=send_sem.at[i], recv_sem=recv_sem.at[i],
            device_id=(at_ctx, at_tp), device_id_type=pl.DeviceIdType.MESH,
        )
        copy.start()
        sent.append(copy)
        return copy

    load_x = local(x_in, xg.at[0])
    load_wk = local(wk_in, wkv.at[:, 0:HD])
    load_wv = local(wv_in, wkv.at[:, HD:2 * HD])
    load_g = local(g_in, gg.at[0])
    load_o = local(o_in, ol)
    load_q = local(q_in, qg.at[0])

    barrier = pltpu.get_barrier_semaphore()
    partners = [(ctx, tp_at(dx, dl)) for dx, dl in tp_peers]
    partners += [(ctx_at(dz, 0, dc), tp) for dz, dc in q_peers]
    partners += [(ctx_at(0, dy, 0), tp) for dy in direct]
    for partner in partners:
        pl.semaphore_signal(barrier, inc=1, device_id=partner, device_id_type=pl.DeviceIdType.MESH)

    pl.semaphore_wait(barrier, len(partners))

    low, high = slice(0, ROWS // 2), slice(ROWS // 2, ROWS)

    def halves(step):
        return (low, high) if step == 1 else (high, low)

    def tp_round(src, buf, dl):
        got = {}
        for turn in range(2):
            for dx in beside(nx):
                part = halves(dx)[turn]
                got[dx, dl, turn] = remote(
                    src.at[part, :], buf.at[dx * nl + dl, part, :], ctx, tp_at(dx, 0)
                )
        return got

    def tp_begin(src, buf):
        got = {}
        if nl > 1:
            got[0, 1] = remote(src, buf.at[1], ctx, tp_at(0, 1))
        got.update(tp_round(src, buf, 0))
        return got

    def tp_partner(buf, got):
        if nl > 1:
            got[0, 1].wait_recv()
            got.update(tp_round(buf.at[1], buf, 1))

    def tp_sides(buf, got, dl):
        for dx in beside(nx):
            got[dx, dl, 0].wait_recv()
            if nx == 4:
                part = halves(dx)[0]
                got[2, dl, dx] = remote(
                    buf.at[dx * nl + dl, part, :], buf.at[2 * nl + dl, part, :], ctx, tp_at(dx, 0)
                )
        for dx in beside(nx):
            got[dx, dl, 1].wait_recv()

    def tp_opposite(got, dl):
        for dx in beside(nx):
            got[2, dl, dx].wait_recv()

    def z_begin(src, buf):
        got = {}
        for turn in range(2):
            for dz in beside(nz):
                part = halves(dz)[turn]
                got[dz, 0, turn] = remote(
                    src.at[part, :], buf.at[2 * dz, part, :], ctx_at(dz, 0, 0), tp
                )
        got[0, 1] = remote(src, buf.at[1], ctx_at(0, 0, 1), tp)
        return got

    def z_sides(buf, got):
        for dz in beside(nz):
            got[dz, 0, 0].wait_recv()
            if nz == 4:
                part = halves(dz)[0]
                got[2, 0, dz] = remote(
                    buf.at[2 * dz, part, :], buf.at[4, part, :], ctx_at(dz, 0, 0), tp
                )

    def z_rest(buf, got):
        for dz in beside(nz):
            got[dz, 0, 1].wait_recv()
            got[dz, 1] = remote(buf.at[2 * dz], buf.at[2 * dz + 1], ctx_at(0, 0, 1), tp)

    def z_opposite(buf, got):
        if nz == 4:
            for dz in beside(nz):
                got[2, 0, dz].wait_recv()
            got[2, 1] = remote(buf.at[4], buf.at[5], ctx_at(0, 0, 1), tp)

    def z_finish(got):
        for dz in range(nz):
            got[dz, 1].wait_recv()

    got_x = tp_begin(x_in, xg)

    order = key_order(ny)
    place = {dy: p for p, dy in enumerate(order)}
    row_id = lax.broadcasted_iota(jnp.int32, (ROWS, HD), 0)
    lane_id = lax.broadcasted_iota(jnp.int32, (1, ROWS), 1)
    for p, dy in enumerate(order):
        at = ctx_at(0, ny - dy, 0)
        first, second = roster[2 * at] * BLOCK, roster[2 * at + 1] * BLOCK
        posk[p * ROWS:(p + 1) * ROWS, :] = row_id + jnp.where(row_id < BLOCK, first, second - BLOCK)
    for j in range(nj):
        at = ctx_at(nz - j // 2, 0, 2 - j % 2)
        first, second = roster[2 * at] * BLOCK, roster[2 * at + 1] * BLOCK
        posq[j:j + 1, :] = lane_id + jnp.where(lane_id < BLOCK, first, second - BLOCK)
    own = place[0]
    angle = posk[own * ROWS:(own + 1) * ROWS, :].astype(jnp.float32) * freq[...]
    cosine = jnp.cos(angle)
    lane = lax.broadcasted_iota(jnp.int32, (ROWS, HD), 1)
    sine = jnp.where(lane < HD // 2, -1.0, 1.0) * jnp.sin(angle)

    load_g.wait()
    load_o.wait()
    for h in range(GROUP):
        cols = slice(h * HD, (h + 1) * HD)
        product = gg[0, :, cols].astype(jnp.float32) * ol[:, cols].astype(jnp.float32)
        delta[0, :, cols] = jnp.sum(product.T, axis=0, keepdims=True)

    def project(dx, dl):
        at = ((xi + nx - dx) % nx) * nl + (zl + nl - dl) % nl
        rows = pl.ds(pl.multiple_of(at * WIDE, WIDE), WIDE)
        return matmul(xg[dx * nl + dl], wkv[rows, :])

    load_x.wait()
    load_wk.wait()
    load_wv.wait()
    raw = project(0, 0)

    tp_partner(xg, got_x)
    got_q = z_begin(q_in, qg)
    tp_sides(xg, got_x, 0)
    if nl > 1:
        raw += project(0, 1)
    for dx in beside(nx):
        raw += project(dx, 0)
    if nl > 1:
        tp_sides(xg, got_x, 1)
    z_sides(qg, got_q)
    if nl > 1:
        for dx in beside(nx):
            raw += project(dx, 1)
    if nx == 4:
        for dl in range(nl):
            tp_opposite(got_x, dl)
            raw += project(2, dl)

    key_raw = raw[:, 0:HD]
    keys = key_raw * cosine + pltpu.roll(key_raw, HD // 2, 1) * sine
    own_rows = pl.ds(own * ROWS, ROWS)
    kv[own_rows, 0:HD] = keys.astype(jnp.bfloat16)
    kv[own_rows, HD:2 * HD] = raw[:, HD:2 * HD].astype(jnp.bfloat16)

    def kv_send(dy_from, dy_to, start=0, count=ROWS):
        src = kv.at[pl.ds(place[dy_from] * ROWS + start, count), :]
        dst = kv.at[pl.ds(place[dy_to] * ROWS + start, count), :]
        return remote(src, dst, ctx_at(0, (ny + dy_to - dy_from) % ny, 0), tp)

    got_kv = {}
    for dy in direct:
        got_kv[dy] = [kv_send(0, dy)]
    z_rest(qg, got_q)
    got_g = z_begin(g_in, gg)
    got_delta = [
        remote(delta.at[0], delta.at[2 * dz + dc], ctx_at(dz, 0, dc), tp) for dz, dc in q_peers
    ]
    load_q.wait()

    def kv_forward():
        if ny == 8:
            got_kv[4] = []
            for dy, onward, start in ((2, 3, 0), (6, 5, ROWS // 2)):
                for copy in got_kv[dy]:
                    copy.wait_recv()
                got_kv[dy] = []
                got_kv[onward] = [kv_send(dy, onward)]
                got_kv[4].append(kv_send(dy, 4, start, ROWS // 2))

    def slot_of(a):
        return ((z + nz - a // 2) % nz) * 2 + (c + 2 - a % 2) % 2

    def place_of(j):
        return ((z + nz - j // 2) % nz) * 2 + (c + 2 - j % 2) % 2

    def score_step(k, a):
        j = slot_of(a)
        rows = pl.ds(pl.multiple_of(k * 2 * ROWS, 2 * ROWS), 2 * ROWS)
        scores = matmul_nt(kv[rows, 0:HD], stacked(qg[j]))
        allowed = posk[rows, :] <= posq[pl.ds(j, 1), :]
        for h in range(GROUP):
            cols = slice(h * HD, (h + 1) * HD)
            part = jnp.where(allowed, scores[:, cols] * (SCALE * LOG2E), NEG)
            top = jnp.maximum(jnp.max(part, axis=0, keepdims=True), FLOOR)
            weight = jnp.exp2(part - top)
            probs[k, j, :, cols] = weight
            peak[k, a, :, cols] = top
            total[k, a, :, cols] = jnp.sum(weight, axis=0, keepdims=True)

    batch = nj // 2

    def send_totals(b):
        for i in range(batch):
            a = b * batch + i
            top = peak[0, a]
            for k in range(1, chunks):
                top = jnp.maximum(top, peak[k, a])
            mass = total[0, a] * jnp.exp2(peak[0, a] - top)
            for k in range(1, chunks):
                mass += total[k, a] * jnp.exp2(peak[k, a] - top)
            lse_own[b, i:i + 1, :] = jnp.where(
                mass > 0.0, top + jnp.log(jnp.maximum(mass, 1e-30)) * LOG2E, NEG
            )
        return [
            remote(lse_own.at[b], lse_got.at[2 * dz + dc, b], ctx_at(dz, 0, dc), tp)
            for dz, dc in q_peers
        ]

    def take_totals(b, got):
        for copy in got:
            copy.wait_recv()
        top = lse_own[b]
        for s in range(1, nj):
            top = jnp.maximum(top, lse_got[s, b])
        mass = jnp.exp2(lse_own[b] - top)
        for s in range(1, nj):
            mass += jnp.exp2(lse_got[s, b] - top)
        lse = top + jnp.log(mass) * LOG2E
        for k in range(chunks):
            for i in range(batch):
                fac[k, b * batch + i] = jnp.exp2(peak[k, b * batch + i] - lse[i:i + 1, :])

    def each(count, step):
        unit = 4 if count % 4 == 0 else 1

        def run(i, carry):
            for u in range(unit):
                step(i * unit + u)
            return carry

        lax.fori_loop(0, count // unit, run, 0)

    mine = pl.ds(pl.multiple_of(c * HD, HD), HD)
    got_w = {}

    def send_weights():
        for dx, dl in [(dx, dl) for dl in reversed(range(nl)) for dx in range(1, nx)]:
            rows = pl.ds(pl.multiple_of(tp_at(dx, dl) * WIDE, WIDE), WIDE)
            s = dx * nl + dl
            got_w[s] = remote(wkv.at[rows, mine], w_cols.at[s, :, mine], ctx, tp_at(dx, 0))

    got_w_sib = {}

    def share_weights():
        for s in got_w:
            got_w[s].wait_recv()
            got_w_sib[s] = remote(
                w_cols.at[s, :, mine], w_cols.at[s, :, mine], ctx_at(0, 0, 1), tp
            )

    def take_keys(k):
        for dy in order[2 * k:2 * k + 2]:
            for copy in got_kv.get(dy, []):
                copy.wait_recv()

    def scores_of(k, slots):
        for j in slots:
            score_step(k, place_of(j))

    late = [4, 5] if nz == 4 else []
    early = [j for j in range(nj) if j not in late]
    z_opposite(qg, got_q)
    got_q[0, 1].wait_recv()
    for dz in beside(nz):
        got_q[dz, 1].wait_recv()
    ahead_of_rest = [k for k in (chunks - 1, chunks - 2) if k > 0]
    if not ahead_of_rest:
        kv_forward()
    for k in ahead_of_rest:
        take_keys(k)
        scores_of(k, early)
        if k == chunks - 1:
            kv_forward()
            send_weights()
    z_sides(gg, got_g)
    if late:
        got_q[2, 1].wait_recv()
        for k in ahead_of_rest:
            scores_of(k, late)
    z_rest(gg, got_g)
    for k in reversed(range(1, max(chunks - 2, 1))):
        take_keys(k)
        each(nj, functools.partial(score_step, k))
    take_keys(0)
    if not ahead_of_rest:
        send_weights()
    got_lse = []
    for b in range(2):
        each(batch, lambda i, first=b * batch: score_step(0, first + i))
        got_lse.append(send_totals(b))
    z_opposite(gg, got_g)
    for k in range(chunks):
        rows = slice(2 * k * ROWS, 2 * (k + 1) * ROWS)
        kt[k] = kv[rows, 0:HD].astype(jnp.float32).T.astype(jnp.bfloat16)
    for copy in got_delta:
        copy.wait_recv()
    z_finish(got_g)

    def first_d_probs(j):
        ahead[j] = matmul_nt(kv[0:2 * ROWS, HD:2 * HD], stacked(gg[j])) - delta[j]

    each(nj, first_d_probs)
    take_totals(0, got_lse[0])

    got_dkv = {}
    got_sib = {}
    def both_cores(dz):
        got_sib[dz].wait_recv()
        return dqt[2 * dz] * SCALE + dq_sib[dz].astype(jnp.float32)

    got_half = {}
    def send_halves():
        if nz != 4:
            return
        dq_snd[2 * nz - 2] = both_cores(2).astype(jnp.bfloat16)
        got_half[1] = remote(dq_snd.at[2 * nz - 2, low, :], dq_half.at[low, :], ctx_at(3, 0, 0), tp)
        got_half[3] = remote(dq_snd.at[2 * nz - 2, high, :], dq_half.at[high, :], ctx_at(1, 0, 0), tp)

    got_relay = {}

    def dkv_send(dy, to, dst, start=0, count=ROWS):
        src = dkv_snd.at[place[dy], pl.ds(start, count), :]
        return remote(src, dst.at[pl.ds(start, count), :], ctx_at(0, (ny + to) % ny, 0), tp)

    for k in range(chunks):
        rows = slice(2 * k * ROWS, 2 * (k + 1) * ROWS)
        acc[...] = jnp.zeros_like(acc)

        def grad_step(j, k=k, rows=rows):
            gs, qs = stacked(gg[j]), stacked(qg[j])
            if k == 0:
                d_probs = ahead[j]
            else:
                d_probs = matmul_nt(kv[rows, HD:2 * HD], gs) - delta[j]
            prob = probs[k, j] * fac[k, place_of(j)]
            d_scores = (prob * d_probs).astype(jnp.bfloat16)
            acc[:, HD:2 * HD] += matmul(prob.astype(jnp.bfloat16), gs)
            acc[:, 0:HD] += matmul(d_scores, qs)
            part = matmul(kt[k], d_scores)
            if k == 0:
                dqt[j] = part
            else:
                dqt[j] += part

        if k == 0:
            each(batch, lambda a, step=grad_step: step(slot_of(a)))
            take_totals(1, got_lse[1])
            each(batch, lambda a, step=grad_step: step(slot_of(batch + a)))
        if 0 < k < chunks - 1:
            each(nj, grad_step)
        if k == chunks - 1:
            if k:
                each(nz, lambda i, step=grad_step: step(2 * i + 1))
            for dz in far_first(nz):
                dq_snd[dz] = (dqt[2 * dz + 1] * SCALE).astype(jnp.bfloat16)
                got_sib[dz] = remote(dq_snd.at[dz], dq_sib.at[dz], ctx_at(0, 0, 1), tp)
            if k:
                for dz in [dz for dz in (2, 1) if dz < nz]:
                    grad_step(2 * dz)
                send_halves()
                for dz in [dz for dz in (3, 0) if dz < nz]:
                    grad_step(2 * dz)
            else:
                send_halves()
        for i, dy in enumerate(order[2 * k:2 * k + 2]):
            if dy == 0:
                continue
            p = 2 * k + i
            part = acc[i * ROWS:(i + 1) * ROWS, :]
            d_key, d_value = part[:, 0:HD] * SCALE, part[:, HD:2 * HD]
            if ny == 8 and dy in (2, 6):
                side, half = (0, low) if dy == 2 else (1, high)
                got_relay[dy].wait_recv()
                got_relay[4, dy].wait_recv()
                d_key += dkv_relay[side, :, 0:HD].astype(jnp.float32)
                d_value += dkv_relay[side, :, HD:2 * HD].astype(jnp.float32)
                more = dkv_relay[2, half, :].astype(jnp.float32)
                none = jnp.zeros_like(more)
                more = jnp.concatenate([more, none] if dy == 2 else [none, more], axis=0)
                d_key += more[:, 0:HD]
                d_value += more[:, HD:2 * HD]
            dkv_snd[p, :, 0:HD] = d_key.astype(jnp.bfloat16)
            dkv_snd[p, :, HD:2 * HD] = d_value.astype(jnp.bfloat16)
            if ny == 8 and dy == 4:
                got_relay[4, 2] = dkv_send(4, -2, dkv_relay.at[2], 0, ROWS // 2)
                got_relay[4, 6] = dkv_send(4, 2, dkv_relay.at[2], ROWS // 2, ROWS // 2)
            elif ny == 8 and dy in (3, 5):
                side = 0 if dy == 3 else 1
                got_relay[2 if dy == 3 else 6] = dkv_send(dy, -1 if dy == 3 else 1, dkv_relay.at[side])
            else:
                got_dkv[dy] = dkv_send(dy, -dy, dkv_got.at[p])
        if k == max(chunks - 2, 0):
            share_weights()

    i = own % 2
    d_key = acc[i * ROWS:(i + 1) * ROWS, 0:HD] * SCALE
    d_value = acc[i * ROWS:(i + 1) * ROWS, HD:2 * HD]
    for dy in got_dkv:
        got_dkv[dy].wait_recv()
        d_key += dkv_got[place[dy], :, 0:HD].astype(jnp.float32)
        d_value += dkv_got[place[dy], :, HD:2 * HD].astype(jnp.float32)
    d_key = d_key * cosine - pltpu.roll(d_key, HD // 2, 1) * sine
    d_kv = jnp.concatenate([d_key, d_value], axis=1).astype(jnp.bfloat16)
    dkv_all[0] = d_kv
    got_all = tp_round(dkv_all.at[0], dkv_all, 0)

    got_dq = {}
    for dz in beside(nz):
        both = both_cores(dz)
        if nz == 4:
            got_half[dz].wait_recv()
            part = low if dz == 1 else high
            other = high if dz == 1 else low
            dq_snd[nz + dz, part, :] = (
                both[part] + dq_half[part, :].astype(jnp.float32)
            ).astype(jnp.bfloat16)
            dq_snd[nz + dz, other, :] = both[other].astype(jnp.bfloat16)
        else:
            dq_snd[nz + dz] = both.astype(jnp.bfloat16)
        got_dq[dz] = remote(dq_snd.at[nz + dz], dq_got.at[dz], ctx_at(nz - dz, 0, 0), tp)
    tp_sides(dkv_all, got_all, 0)
    for s in got_w_sib:
        got_w_sib[s].wait_recv()

    def term(dx, dl):
        if dx == 0:
            weights = wkv[pl.ds(pl.multiple_of(tp_at(0, dl) * WIDE, WIDE), WIDE), :]
        else:
            weights = w_cols[dx * nl + dl]
        return matmul_nt(dkv_all[dx * nl], weights).astype(jnp.bfloat16).astype(jnp.float32)

    def near_terms(dl):
        total = term(0, dl)
        for dx in beside(nx):
            total += term(dx, dl)
        return total

    sums = [near_terms(dl) for dl in reversed(range(nl))]
    if nx == 4:
        tp_opposite(got_all, 0)
    if nl > 1:
        di_snd[...] = (sums[0] + term(2, 1) if nx == 4 else sums[0]).astype(jnp.bfloat16)
        got_di = remote(di_snd, di_got, ctx, tp_at(0, 1))
    d_input = sums[-1] + term(2, 0) if nx == 4 else sums[-1]

    d_query = both_cores(0)
    for dz in beside(nz):
        got_dq[dz].wait_recv()
        d_query += dq_got[dz].astype(jnp.float32)
    for h in range(GROUP):
        cols = slice(h * HD, (h + 1) * HD)
        dq_res[:, cols] = d_query[:, cols].T.astype(jnp.bfloat16)
    store_dq = local(dq_res, dq_out)

    if nl > 1:
        got_di.wait_recv()
        d_input += di_got[...].astype(jnp.float32)
    di_res[...] = d_input.astype(jnp.bfloat16)
    store_di = local(di_res, di_out)
    for copy in sent:
        copy.wait_send()
    store_dq.wait()
    store_di.wait()


def body(grid, x_stash, w_key, w_value, query, out_stash, d_out, roster):
    nz, ny, nx, nl = grid
    nj, nt, chunks = 2 * nz, nx * nl, ny // 2
    bf16, f32 = jnp.bfloat16, jnp.float32
    half = ROPE_BASE ** (-(np.arange(HD // 2) * 2.0) / HD)
    freq = jnp.asarray(np.concatenate([half, half])[None, :].astype(np.float32))
    copies = 160
    vmem = pltpu.VMEM
    hbm = pl.BlockSpec(memory_space=pl.ANY)
    flops = 2 * nj * WIDE * ny * ROWS * HD * 5
    return pl.pallas_call(
        functools.partial(kernel, grid),
        out_shape=(
            jax.ShapeDtypeStruct((ROWS, WIDE), bf16),
            jax.ShapeDtypeStruct((ROWS, WIDE), bf16),
        ),
        in_specs=[hbm] * 6
        + [pl.BlockSpec(memory_space=pltpu.SMEM), pl.BlockSpec(memory_space=pltpu.VMEM)],
        out_specs=(hbm, hbm),
        scratch_shapes=[
            vmem((nt, ROWS, WIDE), bf16),
            vmem((nt * WIDE, 2 * HD), bf16),
            vmem((nj, ROWS, WIDE), bf16),
            vmem((nj, ROWS, WIDE), bf16),
            vmem((ROWS, WIDE), bf16),
            vmem((ny * ROWS, 2 * HD), bf16),
            vmem((chunks, HD, 2 * ROWS), bf16),
            vmem((ny * ROWS, HD), jnp.int32),
            vmem((nj, ROWS), jnp.int32),
            vmem((chunks, nj, 2 * ROWS, WIDE), f32),
            vmem((chunks, nj, 1, WIDE), f32),
            vmem((chunks, nj, 1, WIDE), f32),
            vmem((chunks, nj, 1, WIDE), f32),
            vmem((2, nz, WIDE), f32),
            vmem((nj, 2, nz, WIDE), f32),
            vmem((nj, 1, WIDE), f32),
            vmem((nj, 2 * ROWS, WIDE), f32),
            vmem((nj, HD, WIDE), f32),
            vmem((2 * nz, HD, WIDE), bf16),
            vmem((nz, HD, WIDE), bf16),
            vmem((HD, WIDE), bf16),
            vmem((nz, HD, WIDE), bf16),
            vmem((2 * ROWS, 2 * HD), f32),
            vmem((ny, ROWS, 2 * HD), bf16),
            vmem((3, ROWS, 2 * HD), bf16),
            vmem((ny, ROWS, 2 * HD), bf16),
            vmem((nt, ROWS, 2 * HD), bf16),
            vmem((nt, WIDE, 2 * HD), bf16),
            vmem((ROWS, WIDE), bf16),
            vmem((ROWS, WIDE), bf16),
            vmem((ROWS, WIDE), bf16),
            vmem((ROWS, WIDE), bf16),
            pltpu.SemaphoreType.DMA((copies,)),
            pltpu.SemaphoreType.DMA((copies,)),
            pltpu.SemaphoreType.DMA((8,)),
        ],
        compiler_params=pltpu.CompilerParams(
            collective_id=0, has_side_effects=True, vmem_limit_bytes=56 * 1024 * 1024
        ),
        cost_estimate=pl.CostEstimate(
            flops=flops, bytes_accessed=4 * 1024 * 1024, transcendentals=nj * WIDE * ny * ROWS
        ),
    )(x_stash, w_key, w_value, query, out_stash, d_out, roster, freq)


def solution(mesh):
    grid = GRIDS[mesh.shape["ctx"], mesh.shape["tp"]]
    split = P("ctx", "tp")
    return jax.shard_map(
        functools.partial(body, grid),
        mesh=mesh,
        in_specs=(split, P(None, "tp"), P(None, "tp"), split, split, split, P()),
        out_specs=(split, split),
        check_vma=False,
    )
```

```python
import functools

import jax
import jax.numpy as jnp
import numpy as np
from jax import lax
from jax.experimental import pallas as pl
from jax.experimental.pallas import tpu as pltpu
from jax.sharding import PartitionSpec as P

HD = 128
GROUP = 4
BLOCK = 64
ROWS = 128
WIDE = GROUP * HD
ROPE_BASE = 500000.0
SCALE = HD ** -0.5
LOG2E = 1.4426950408889634
NEG = -1e30
FLOOR = -1e20

GRIDS = {(64, 8): (4, 8, 4, 2)}

NT = (((1,), (1,)), ((), ()))


def matmul_nt(a, b):
    return lax.dot_general(a, b, NT, preferred_element_type=jnp.float32)


def matmul(a, b):
    return jnp.dot(a, b, preferred_element_type=jnp.float32)


def stacked(block):
    return jnp.concatenate([block[:, h * HD:(h + 1) * HD] for h in range(GROUP)], axis=0)


def far_first(count):
    return sorted(range(count), key=lambda d: (-min(d, count - d), d))


def key_order(ny):
    return [4, 3, 5, 7, 2, 6, 1, 0] if ny == 8 else far_first(ny)


def beside(count):
    return sorted({1 % count, count - 1} - {0})


def kernel(
    grid, x_in, wk_in, wv_in, q_in, o_in, g_in, roster, freq,
    dq_out, di_out,
    xg, wkv, qg, gg, ol, kv, kt, posk, posq, probs, peak, total, fac, lse_own, lse_got,
    delta, ahead, dqt, dq_snd, dq_sib, dq_half, dq_got, acc, held, dkv_snd, dkv_relay, dkv_got, dkv_all, w_cols, di_snd, di_got,
    send_sem, recv_sem, local_sem,
):
    nz, ny, nx, nl = grid
    nj = 2 * nz
    chunks = ny // 2
    ctx, tp = lax.axis_index("ctx"), lax.axis_index("tp")
    z, y, c = ctx // (2 * ny), (ctx // 2) % ny, ctx % 2
    xi, zl = tp // nl, tp % nl

    def ctx_at(dz, dy, dc):
        return (((z + dz) % nz) * ny + (y + dy) % ny) * 2 + (c + dc) % 2

    def tp_at(dx, dl):
        return ((xi + dx) % nx) * nl + (zl + dl) % nl

    tp_peers = [(dx, 0) for dx in range(1, nx)] + [(0, dl) for dl in range(1, nl)]
    q_peers = [(dz, dc) for dz in range(nz) for dc in range(2) if (dz, dc) != (0, 0)]
    direct = [1, 7, 2, 6] if ny == 8 else list(range(1, ny))

    used = [0, 0]

    def local(src, dst):
        copy = pltpu.make_async_copy(src, dst, local_sem.at[used[0]])
        used[0] += 1
        copy.start()
        return copy

    sent = []

    def remote(src, dst, at_ctx, at_tp):
        i = used[1]
        used[1] += 1
        copy = pltpu.make_async_remote_copy(
            src_ref=src, dst_ref=dst, send_sem=send_sem.at[i], recv_sem=recv_sem.at[i],
            device_id=(at_ctx, at_tp), device_id_type=pl.DeviceIdType.MESH,
        )
        copy.start()
        sent.append(copy)
        return copy

    load_x = local(x_in, xg.at[0])
    load_wk = local(wk_in, wkv.at[:, 0:HD])
    load_wv = local(wv_in, wkv.at[:, HD:2 * HD])
    load_g = local(g_in, gg.at[0])
    load_o = local(o_in, ol)
    load_q = local(q_in, qg.at[0])

    barrier = pltpu.get_barrier_semaphore()
    partners = [(ctx, tp_at(dx, dl)) for dx, dl in tp_peers]
    partners += [(ctx_at(dz, 0, dc), tp) for dz, dc in q_peers]
    partners += [(ctx_at(0, dy, 0), tp) for dy in direct]
    for partner in partners:
        pl.semaphore_signal(barrier, inc=1, device_id=partner, device_id_type=pl.DeviceIdType.MESH)

    pl.semaphore_wait(barrier, len(partners))

    low, high = slice(0, ROWS // 2), slice(ROWS // 2, ROWS)

    def halves(step):
        return (low, high) if step == 1 else (high, low)

    def tp_round(src, buf, dl):
        got = {}
        for turn in range(2):
            for dx in beside(nx):
                part = halves(dx)[turn]
                got[dx, dl, turn] = remote(
                    src.at[part, :], buf.at[dx * nl + dl, part, :], ctx, tp_at(dx, 0)
                )
        return got

    def tp_begin(src, buf):
        got = {}
        if nl > 1:
            for turn, part in enumerate((low, high)):
                got[0, 1, turn] = remote(src.at[part, :], buf.at[1, part, :], ctx, tp_at(0, 1))
        got.update(tp_round(src, buf, 0))
        return got

    def tp_partner(buf, got):
        if nl > 1:
            for turn, part in enumerate((low, high)):
                got[0, 1, turn].wait_recv()
                for dx in beside(nx):
                    got[dx, 1, turn if halves(dx)[0] is low else 1 - turn] = remote(
                        buf.at[1, part, :], buf.at[dx * nl + 1, part, :], ctx, tp_at(dx, 0)
                    )

    def tp_sides(buf, got, dl):
        for dx in beside(nx):
            got[dx, dl, 0].wait_recv()
            if nx == 4:
                part = halves(dx)[0]
                got[2, dl, dx] = remote(
                    buf.at[dx * nl + dl, part, :], buf.at[2 * nl + dl, part, :], ctx, tp_at(dx, 0)
                )
        for dx in beside(nx):
            got[dx, dl, 1].wait_recv()

    def tp_opposite(got, dl):
        for dx in beside(nx):
            got[2, dl, dx].wait_recv()

    def z_begin(src, buf):
        got = {}
        for turn in range(2):
            for dz in beside(nz):
                part = halves(dz)[turn]
                got[dz, 0, turn] = remote(
                    src.at[part, :], buf.at[2 * dz, part, :], ctx_at(dz, 0, 0), tp
                )
        got[0, 1] = remote(src, buf.at[1], ctx_at(0, 0, 1), tp)
        return got

    def z_sides(buf, got):
        for dz in beside(nz):
            got[dz, 0, 0].wait_recv()
            if nz == 4:
                part = halves(dz)[0]
                got[2, 0, dz] = remote(
                    buf.at[2 * dz, part, :], buf.at[4, part, :], ctx_at(dz, 0, 0), tp
                )

    def z_rest(buf, got):
        for dz in beside(nz):
            got[dz, 0, 1].wait_recv()
            got[dz, 1] = remote(buf.at[2 * dz], buf.at[2 * dz + 1], ctx_at(0, 0, 1), tp)

    def z_opposite(buf, got):
        if nz == 4:
            for dz in beside(nz):
                got[2, 0, dz].wait_recv()
            got[2, 1] = remote(buf.at[4], buf.at[5], ctx_at(0, 0, 1), tp)

    def z_finish(got):
        for dz in range(nz):
            got[dz, 1].wait_recv()

    got_x = tp_begin(x_in, xg)

    order = key_order(ny)
    place = {dy: p for p, dy in enumerate(order)}
    row_id = lax.broadcasted_iota(jnp.int32, (ROWS, HD), 0)
    lane_id = lax.broadcasted_iota(jnp.int32, (1, ROWS), 1)
    for p, dy in enumerate(order):
        at = ctx_at(0, ny - dy, 0)
        first, second = roster[2 * at] * BLOCK, roster[2 * at + 1] * BLOCK
        posk[p * ROWS:(p + 1) * ROWS, :] = row_id + jnp.where(row_id < BLOCK, first, second - BLOCK)
    for j in range(nj):
        at = ctx_at(nz - j // 2, 0, 2 - j % 2)
        first, second = roster[2 * at] * BLOCK, roster[2 * at + 1] * BLOCK
        posq[j:j + 1, :] = lane_id + jnp.where(lane_id < BLOCK, first, second - BLOCK)
    own = place[0]
    angle = posk[own * ROWS:(own + 1) * ROWS, :].astype(jnp.float32) * freq[...]
    cosine = jnp.cos(angle)
    lane = lax.broadcasted_iota(jnp.int32, (ROWS, HD), 1)
    sine = jnp.where(lane < HD // 2, -1.0, 1.0) * jnp.sin(angle)

    load_g.wait()
    load_o.wait()
    for h in range(GROUP):
        cols = slice(h * HD, (h + 1) * HD)
        product = gg[0, :, cols].astype(jnp.float32) * ol[:, cols].astype(jnp.float32)
        delta[0, :, cols] = jnp.sum(product.T, axis=0, keepdims=True)

    def project(dx, dl):
        at = ((xi + nx - dx) % nx) * nl + (zl + nl - dl) % nl
        rows = pl.ds(pl.multiple_of(at * WIDE, WIDE), WIDE)
        return matmul(xg[dx * nl + dl], wkv[rows, :])

    load_x.wait()
    load_wk.wait()
    load_wv.wait()
    raw = project(0, 0)

    if nl > 1:
        for turn in range(2):
            got_x[0, 1, turn].wait_send()
            sent.remove(got_x[0, 1, turn])
    got_q = z_begin(q_in, qg)
    tp_partner(xg, got_x)
    tp_sides(xg, got_x, 0)
    if nl > 1:
        raw += project(0, 1)
    for dx in beside(nx):
        raw += project(dx, 0)
    if nl > 1:
        tp_sides(xg, got_x, 1)
    z_sides(qg, got_q)
    if nl > 1:
        for dx in beside(nx):
            raw += project(dx, 1)
    if nx == 4:
        for dl in range(nl):
            tp_opposite(got_x, dl)
            raw += project(2, dl)

    key_raw = raw[:, 0:HD]
    keys = key_raw * cosine + pltpu.roll(key_raw, HD // 2, 1) * sine
    own_rows = pl.ds(own * ROWS, ROWS)
    kv[own_rows, 0:HD] = keys.astype(jnp.bfloat16)
    kv[own_rows, HD:2 * HD] = raw[:, HD:2 * HD].astype(jnp.bfloat16)

    def kv_send(dy_from, dy_to, start=0, count=ROWS):
        src = kv.at[pl.ds(place[dy_from] * ROWS + start, count), :]
        dst = kv.at[pl.ds(place[dy_to] * ROWS + start, count), :]
        return remote(src, dst, ctx_at(0, (ny + dy_to - dy_from) % ny, 0), tp)

    got_kv = {}
    for dy in direct:
        got_kv[dy] = [kv_send(0, dy)]
    z_rest(qg, got_q)
    got_g = z_begin(g_in, gg)
    got_delta = [
        remote(delta.at[0], delta.at[2 * dz + dc], ctx_at(dz, 0, dc), tp) for dz, dc in q_peers
    ]
    load_q.wait()

    def kv_forward():
        if ny == 8:
            got_kv[4] = []
            for dy, onward, start in ((2, 3, 0), (6, 5, ROWS // 2)):
                for copy in got_kv[dy]:
                    copy.wait_recv()
                got_kv[dy] = []
                got_kv[onward] = [kv_send(dy, onward)]
                got_kv[4].append(kv_send(dy, 4, start, ROWS // 2))

    def slot_of(a):
        return ((z + nz - a // 2) % nz) * 2 + (c + 2 - a % 2) % 2

    def place_of(j):
        return ((z + nz - j // 2) % nz) * 2 + (c + 2 - j % 2) % 2

    def score_step(k, a):
        j = slot_of(a)
        rows = pl.ds(pl.multiple_of(k * 2 * ROWS, 2 * ROWS), 2 * ROWS)
        scores = matmul_nt(kv[rows, 0:HD], stacked(qg[j]))
        allowed = posk[rows, :] <= posq[pl.ds(j, 1), :]
        for h in range(GROUP):
            cols = slice(h * HD, (h + 1) * HD)
            part = jnp.where(allowed, scores[:, cols] * (SCALE * LOG2E), NEG)
            top = jnp.maximum(jnp.max(part, axis=0, keepdims=True), FLOOR)
            weight = jnp.exp2(part - top)
            probs[k, j, :, cols] = weight
            peak[k, a, :, cols] = top
            total[k, a, :, cols] = jnp.sum(weight, axis=0, keepdims=True)

    batch = nj // 2

    def send_totals(b):
        for i in range(batch):
            a = b * batch + i
            top = peak[0, a]
            for k in range(1, chunks):
                top = jnp.maximum(top, peak[k, a])
            mass = total[0, a] * jnp.exp2(peak[0, a] - top)
            for k in range(1, chunks):
                mass += total[k, a] * jnp.exp2(peak[k, a] - top)
            lse_own[b, i:i + 1, :] = jnp.where(
                mass > 0.0, top + jnp.log(jnp.maximum(mass, 1e-30)) * LOG2E, NEG
            )
        return [
            remote(lse_own.at[b], lse_got.at[2 * dz + dc, b], ctx_at(dz, 0, dc), tp)
            for dz, dc in q_peers
        ]

    def take_totals(b, got):
        for copy in got:
            copy.wait_recv()
        top = lse_own[b]
        for s in range(1, nj):
            top = jnp.maximum(top, lse_got[s, b])
        mass = jnp.exp2(lse_own[b] - top)
        for s in range(1, nj):
            mass += jnp.exp2(lse_got[s, b] - top)
        lse = top + jnp.log(mass) * LOG2E
        for k in range(chunks):
            for i in range(batch):
                fac[k, b * batch + i] = jnp.exp2(peak[k, b * batch + i] - lse[i:i + 1, :])

    def each(count, step):
        unit = 4 if count % 4 == 0 else 1

        def run(i, carry):
            for u in range(unit):
                step(i * unit + u)
            return carry

        lax.fori_loop(0, count // unit, run, 0)

    mine = pl.ds(pl.multiple_of(c * HD, HD), HD)
    got_w = {}

    blocks = [(dx, dl) for dl in reversed(range(nl)) for dx in range(1, nx)]

    def send_weights():
        for dx, dl in blocks:
            rows = pl.ds(pl.multiple_of(tp_at(dx, dl) * WIDE, WIDE), WIDE)
            s = dx * nl + dl
            got_w[s] = remote(wkv.at[rows, mine], w_cols.at[s, :, mine], ctx, tp_at(dx, 0))

    got_w_sib = {}

    def share_weights():
        for s in got_w:
            got_w[s].wait_recv()
            got_w_sib[s] = remote(
                w_cols.at[s, :, mine], w_cols.at[s, :, mine], ctx_at(0, 0, 1), tp
            )

    def take_keys(k):
        for dy in order[2 * k:2 * k + 2]:
            for copy in got_kv.get(dy, []):
                copy.wait_recv()

    def scores_of(k, slots):
        for j in slots:
            score_step(k, place_of(j))

    late = [4, 5] if nz == 4 else []
    early = [j for j in range(nj) if j not in late]
    z_opposite(qg, got_q)
    got_q[0, 1].wait_recv()
    for dz in beside(nz):
        got_q[dz, 1].wait_recv()
    ahead_of_rest = [k for k in (chunks - 1, chunks - 2) if k > 0]
    if not ahead_of_rest:
        kv_forward()
    for k in ahead_of_rest:
        take_keys(k)
        scores_of(k, early)
        if k == chunks - 1:
            kv_forward()
            send_weights()
    z_sides(gg, got_g)
    if late:
        got_q[2, 1].wait_recv()
        for k in ahead_of_rest:
            scores_of(k, late)
    z_rest(gg, got_g)
    for k in reversed(range(1, max(chunks - 2, 1))):
        take_keys(k)
        each(nj, functools.partial(score_step, k))
    take_keys(0)
    if not ahead_of_rest:
        send_weights()
    got_lse = []
    for b in range(2):
        each(batch, lambda i, first=b * batch: score_step(0, first + i))
        got_lse.append(send_totals(b))
    z_opposite(gg, got_g)
    for k in range(chunks):
        rows = slice(2 * k * ROWS, 2 * (k + 1) * ROWS)
        kt[k] = kv[rows, 0:HD].astype(jnp.float32).T.astype(jnp.bfloat16)
    for copy in got_delta:
        copy.wait_recv()
    z_finish(got_g)

    def first_d_probs(k, j):
        rows = slice(2 * k * ROWS, 2 * (k + 1) * ROWS)
        ahead[k, j] = matmul_nt(kv[rows, HD:2 * HD], stacked(gg[j])) - delta[j]

    for k in range(min(2, chunks)):
        each(nj, functools.partial(first_d_probs, k))
    take_totals(0, got_lse[0])

    got_dkv = {}
    got_sib = {}
    def both_cores(dz):
        got_sib[dz].wait_recv()
        return dqt[2 * dz] * SCALE + dq_sib[dz].astype(jnp.float32)

    got_half = {}
    def send_halves():
        if nz != 4:
            return
        dq_snd[2 * nz - 2] = both_cores(2).astype(jnp.bfloat16)
        got_half[1] = remote(dq_snd.at[2 * nz - 2, low, :], dq_half.at[low, :], ctx_at(3, 0, 0), tp)
        got_half[3] = remote(dq_snd.at[2 * nz - 2, high, :], dq_half.at[high, :], ctx_at(1, 0, 0), tp)

    got_relay = {}

    def dkv_send(dy, to, dst, start=0, count=ROWS):
        src = dkv_snd.at[place[dy], pl.ds(start, count), :]
        return remote(src, dst.at[pl.ds(start, count), :], ctx_at(0, (ny + to) % ny, 0), tp)

    def send_held():
        if ny != 8:
            return
        for i, (dy, half) in enumerate(((2, low), (6, high))):
            p = place[dy]
            got_relay[dy].wait_recv()
            got_relay[4, dy].wait_recv()
            part = held[i] + dkv_relay[i].astype(jnp.float32)
            rest = high if half is low else low
            dkv_snd[p, half, :] = (
                part[half] + dkv_relay[2, half, :].astype(jnp.float32)
            ).astype(jnp.bfloat16)
            dkv_snd[p, rest, :] = part[rest].astype(jnp.bfloat16)
            got_dkv[dy] = dkv_send(dy, -dy, dkv_got.at[p])

    for k in range(chunks):
        rows = slice(2 * k * ROWS, 2 * (k + 1) * ROWS)
        acc[...] = jnp.zeros_like(acc)

        def grad_step(j, k=k, rows=rows):
            gs, qs = stacked(gg[j]), stacked(qg[j])
            if k < 2:
                d_probs = ahead[k, j]
            else:
                d_probs = matmul_nt(kv[rows, HD:2 * HD], gs) - delta[j]
            prob = probs[k, j] * fac[k, place_of(j)]
            d_scores = (prob * d_probs).astype(jnp.bfloat16)
            acc[:, HD:2 * HD] += matmul(prob.astype(jnp.bfloat16), gs)
            acc[:, 0:HD] += matmul(d_scores, qs)
            part = matmul(kt[k], d_scores)
            if k == 0:
                dqt[j] = part
            else:
                dqt[j] += part

        if k == 0:
            each(batch, lambda a, step=grad_step: step(slot_of(a)))
            take_totals(1, got_lse[1])
            each(batch, lambda a, step=grad_step: step(slot_of(batch + a)))
        if 0 < k < chunks - 1:
            each(nj, grad_step)
        if k == chunks - 1:
            if k:
                each(nz, lambda i, step=grad_step: step(2 * i + 1))
            send_held()
            for dz in far_first(nz):
                dq_snd[dz] = (dqt[2 * dz + 1] * SCALE).astype(jnp.bfloat16)
                got_sib[dz] = remote(dq_snd.at[dz], dq_sib.at[dz], ctx_at(0, 0, 1), tp)
            if k:
                each(nz, lambda i, step=grad_step: step(2 * i))
        for i, dy in enumerate(order[2 * k:2 * k + 2]):
            if dy == 0:
                continue
            p = 2 * k + i
            part = acc[i * ROWS:(i + 1) * ROWS, :]
            d_key, d_value = part[:, 0:HD] * SCALE, part[:, HD:2 * HD]
            if ny == 8 and dy in (2, 6):
                held[i, :, 0:HD] = d_key
                held[i, :, HD:2 * HD] = d_value
                continue
            dkv_snd[p, :, 0:HD] = d_key.astype(jnp.bfloat16)
            dkv_snd[p, :, HD:2 * HD] = d_value.astype(jnp.bfloat16)
            if ny == 8 and dy == 4:
                got_relay[4, 2] = dkv_send(4, -2, dkv_relay.at[2], 0, ROWS // 2)
                got_relay[4, 6] = dkv_send(4, 2, dkv_relay.at[2], ROWS // 2, ROWS // 2)
            elif ny == 8 and dy in (3, 5):
                side = 0 if dy == 3 else 1
                got_relay[2 if dy == 3 else 6] = dkv_send(dy, -1 if dy == 3 else 1, dkv_relay.at[side])
            else:
                got_dkv[dy] = dkv_send(dy, -dy, dkv_got.at[p])
        if k == max(chunks - 2, 0):
            share_weights()
        if k == chunks - 1:
            send_halves()

    i = own % 2
    d_key = acc[i * ROWS:(i + 1) * ROWS, 0:HD] * SCALE
    d_value = acc[i * ROWS:(i + 1) * ROWS, HD:2 * HD]
    for dy in got_dkv:
        got_dkv[dy].wait_recv()
        d_key += dkv_got[place[dy], :, 0:HD].astype(jnp.float32)
        d_value += dkv_got[place[dy], :, HD:2 * HD].astype(jnp.float32)
    d_key = d_key * cosine - pltpu.roll(d_key, HD // 2, 1) * sine
    d_kv = jnp.concatenate([d_key, d_value], axis=1).astype(jnp.bfloat16)
    dkv_all[0] = d_kv
    got_all = tp_round(dkv_all.at[0], dkv_all, 0)

    got_dq = {}
    for dz in beside(nz):
        both = both_cores(dz)
        if nz == 4:
            got_half[dz].wait_recv()
            part = low if dz == 1 else high
            other = high if dz == 1 else low
            dq_snd[nz + dz, part, :] = (
                both[part] + dq_half[part, :].astype(jnp.float32)
            ).astype(jnp.bfloat16)
            dq_snd[nz + dz, other, :] = both[other].astype(jnp.bfloat16)
        else:
            dq_snd[nz + dz] = both.astype(jnp.bfloat16)
        got_dq[dz] = remote(dq_snd.at[nz + dz], dq_got.at[dz], ctx_at(nz - dz, 0, 0), tp)
    tp_sides(dkv_all, got_all, 0)
    for s in got_w_sib:
        got_w_sib[s].wait_recv()

    def term(dx, dl):
        if dx == 0:
            weights = wkv[pl.ds(pl.multiple_of(tp_at(0, dl) * WIDE, WIDE), WIDE), :]
        else:
            weights = w_cols[dx * nl + dl]
        return matmul_nt(dkv_all[dx * nl], weights).astype(jnp.bfloat16).astype(jnp.float32)

    def near_terms(dl):
        total = term(0, dl)
        for dx in beside(nx):
            total += term(dx, dl)
        return total

    sums = [near_terms(dl) for dl in reversed(range(nl))]
    if nx == 4:
        tp_opposite(got_all, 0)
    if nl > 1:
        di_snd[...] = (sums[0] + term(2, 1) if nx == 4 else sums[0]).astype(jnp.bfloat16)
        got_di = remote(di_snd, di_got, ctx, tp_at(0, 1))
    d_input = sums[-1] + term(2, 0) if nx == 4 else sums[-1]

    d_query = both_cores(0)
    for dz in beside(nz):
        got_dq[dz].wait_recv()
        d_query += dq_got[dz].astype(jnp.float32)
    for h in range(GROUP):
        cols = slice(h * HD, (h + 1) * HD)
        dq_out[:, cols] = d_query[:, cols].T.astype(jnp.bfloat16)

    if nl > 1:
        got_di.wait_recv()
        d_input += di_got[...].astype(jnp.float32)
    di_out[...] = d_input.astype(jnp.bfloat16)
    for copy in sent:
        copy.wait_send()


def body(grid, x_stash, w_key, w_value, query, out_stash, d_out, roster):
    nz, ny, nx, nl = grid
    nj, nt, chunks = 2 * nz, nx * nl, ny // 2
    bf16, f32 = jnp.bfloat16, jnp.float32
    half = ROPE_BASE ** (-(np.arange(HD // 2) * 2.0) / HD)
    freq = jnp.asarray(np.concatenate([half, half])[None, :].astype(np.float32))
    copies = 160
    vmem = pltpu.VMEM
    hbm = pl.BlockSpec(memory_space=pl.ANY)
    flops = 2 * nj * WIDE * ny * ROWS * HD * 5
    return pl.pallas_call(
        functools.partial(kernel, grid),
        out_shape=(vmem((ROWS, WIDE), bf16), vmem((ROWS, WIDE), bf16)),
        in_specs=[hbm] * 6
        + [pl.BlockSpec(memory_space=pltpu.SMEM), pl.BlockSpec(memory_space=pltpu.VMEM)],
        out_specs=(pl.BlockSpec(memory_space=vmem), pl.BlockSpec(memory_space=vmem)),
        scratch_shapes=[
            vmem((nt, ROWS, WIDE), bf16),
            vmem((nt * WIDE, 2 * HD), bf16),
            vmem((nj, ROWS, WIDE), bf16),
            vmem((nj, ROWS, WIDE), bf16),
            vmem((ROWS, WIDE), bf16),
            vmem((ny * ROWS, 2 * HD), bf16),
            vmem((chunks, HD, 2 * ROWS), bf16),
            vmem((ny * ROWS, HD), jnp.int32),
            vmem((nj, ROWS), jnp.int32),
            vmem((chunks, nj, 2 * ROWS, WIDE), f32),
            vmem((chunks, nj, 1, WIDE), f32),
            vmem((chunks, nj, 1, WIDE), f32),
            vmem((chunks, nj, 1, WIDE), f32),
            vmem((2, nz, WIDE), f32),
            vmem((nj, 2, nz, WIDE), f32),
            vmem((nj, 1, WIDE), f32),
            vmem((min(2, chunks), nj, 2 * ROWS, WIDE), f32),
            vmem((nj, HD, WIDE), f32),
            vmem((2 * nz, HD, WIDE), bf16),
            vmem((nz, HD, WIDE), bf16),
            vmem((HD, WIDE), bf16),
            vmem((nz, HD, WIDE), bf16),
            vmem((2 * ROWS, 2 * HD), f32),
            vmem((2, ROWS, 2 * HD), f32),
            vmem((ny, ROWS, 2 * HD), bf16),
            vmem((3, ROWS, 2 * HD), bf16),
            vmem((ny, ROWS, 2 * HD), bf16),
            vmem((nt, ROWS, 2 * HD), bf16),
            vmem((nt, WIDE, 2 * HD), bf16),
            vmem((ROWS, WIDE), bf16),
            vmem((ROWS, WIDE), bf16),
            pltpu.SemaphoreType.DMA((copies,)),
            pltpu.SemaphoreType.DMA((copies,)),
            pltpu.SemaphoreType.DMA((8,)),
        ],
        compiler_params=pltpu.CompilerParams(
            collective_id=0, has_side_effects=True, vmem_limit_bytes=56 * 1024 * 1024
        ),
        cost_estimate=pl.CostEstimate(
            flops=flops, bytes_accessed=4 * 1024 * 1024, transcendentals=nj * WIDE * ny * ROWS
        ),
    )(x_stash, w_key, w_value, query, out_stash, d_out, roster, freq)


def solution(mesh):
    grid = GRIDS[mesh.shape["ctx"], mesh.shape["tp"]]
    split = P("ctx", "tp")
    return jax.shard_map(
        functools.partial(body, grid),
        mesh=mesh,
        in_specs=(split, P(None, "tp"), P(None, "tp"), split, split, split, P()),
        out_specs=(split, split),
        check_vma=False,
    )
```

```python
import functools

import jax
import jax.numpy as jnp
import numpy as np
from jax import lax
from jax.experimental import pallas as pl
from jax.experimental.pallas import tpu as pltpu
from jax.sharding import PartitionSpec as P

HD = 128
GROUP = 4
BLOCK = 64
ROWS = 128
WIDE = GROUP * HD
ROPE_BASE = 500000.0
SCALE = HD ** -0.5
LOG2E = 1.4426950408889634
NEG = -1e30
FLOOR = -1e20

GRIDS = {(64, 8): (4, 8, 4, 2)}

NT = (((1,), (1,)), ((), ()))


def matmul_nt(a, b):
    return lax.dot_general(a, b, NT, preferred_element_type=jnp.float32)


def matmul(a, b):
    return jnp.dot(a, b, preferred_element_type=jnp.float32)


def stacked(block):
    return jnp.concatenate([block[:, h * HD:(h + 1) * HD] for h in range(GROUP)], axis=0)


def far_first(count):
    return sorted(range(count), key=lambda d: (-min(d, count - d), d))


def key_order(ny):
    return [4, 3, 5, 7, 2, 6, 1, 0] if ny == 8 else far_first(ny)


def beside(count):
    return sorted({1 % count, count - 1} - {0})


def kernel(
    grid, x_in, wk_in, wv_in, q_in, o_in, g_in, roster, freq,
    dq_out, di_out,
    xg, wkv, qg, gg, ol, kv, kt, posk, posq, probs, peak, total, fac, lse_own, lse_got,
    delta, ahead, dqt, dq_snd, dq_sib, dq_half, dq_got, acc, held, dkv_snd, dkv_relay, dkv_got, dkv_all, w_cols, di_snd, di_got,
    send_sem, recv_sem, local_sem,
):
    nz, ny, nx, nl = grid
    nj = 2 * nz
    chunks = ny // 2
    ctx, tp = lax.axis_index("ctx"), lax.axis_index("tp")
    z, y, c = ctx // (2 * ny), (ctx // 2) % ny, ctx % 2
    xi, zl = tp // nl, tp % nl

    def ctx_at(dz, dy, dc):
        return (((z + dz) % nz) * ny + (y + dy) % ny) * 2 + (c + dc) % 2

    def tp_at(dx, dl):
        return ((xi + dx) % nx) * nl + (zl + dl) % nl

    tp_peers = [(dx, 0) for dx in range(1, nx)] + [(0, dl) for dl in range(1, nl)]
    q_peers = [(dz, dc) for dz in range(nz) for dc in range(2) if (dz, dc) != (0, 0)]
    direct = [1, 7, 2, 6] if ny == 8 else list(range(1, ny))

    used = [0, 0]

    def local(src, dst):
        copy = pltpu.make_async_copy(src, dst, local_sem.at[used[0]])
        used[0] += 1
        copy.start()
        return copy

    sent = []

    def remote(src, dst, at_ctx, at_tp):
        i = used[1]
        used[1] += 1
        copy = pltpu.make_async_remote_copy(
            src_ref=src, dst_ref=dst, send_sem=send_sem.at[i], recv_sem=recv_sem.at[i],
            device_id=(at_ctx, at_tp), device_id_type=pl.DeviceIdType.MESH,
        )
        copy.start()
        sent.append(copy)
        return copy

    barrier = pltpu.get_barrier_semaphore()
    partners = [(ctx, tp_at(dx, dl)) for dx, dl in tp_peers]
    partners += [(ctx_at(dz, 0, dc), tp) for dz, dc in q_peers]
    partners += [(ctx_at(0, dy, 0), tp) for dy in direct]
    for partner in partners:
        pl.semaphore_signal(barrier, inc=1, device_id=partner, device_id_type=pl.DeviceIdType.MESH)

    load_x = local(x_in, xg.at[0])
    load_wk = local(wk_in, wkv.at[:, 0:HD])
    load_wv = local(wv_in, wkv.at[:, HD:2 * HD])
    load_g = local(g_in, gg.at[0])
    load_o = local(o_in, ol)
    load_q = local(q_in, qg.at[0])

    pl.semaphore_wait(barrier, len(partners))

    low, high = slice(0, ROWS // 2), slice(ROWS // 2, ROWS)

    def halves(step):
        return (low, high) if step == 1 else (high, low)

    def tp_round(src, buf, dl):
        got = {}
        for turn in range(2):
            for dx in beside(nx):
                part = halves(dx)[turn]
                got[dx, dl, turn] = remote(
                    src.at[part, :], buf.at[dx * nl + dl, part, :], ctx, tp_at(dx, 0)
                )
        return got

    def tp_begin(src, buf):
        got = {}
        if nl > 1:
            for turn, part in enumerate((low, high)):
                got[0, 1, turn] = remote(src.at[part, :], buf.at[1, part, :], ctx, tp_at(0, 1))
        got.update(tp_round(src, buf, 0))
        return got

    def tp_partner(buf, got):
        if nl > 1:
            for turn, part in enumerate((low, high)):
                got[0, 1, turn].wait_recv()
                for dx in beside(nx):
                    got[dx, 1, turn if halves(dx)[0] is low else 1 - turn] = remote(
                        buf.at[1, part, :], buf.at[dx * nl + 1, part, :], ctx, tp_at(dx, 0)
                    )

    def tp_sides(buf, got, dl):
        for dx in beside(nx):
            got[dx, dl, 0].wait_recv()
            if nx == 4:
                part = halves(dx)[0]
                got[2, dl, dx] = remote(
                    buf.at[dx * nl + dl, part, :], buf.at[2 * nl + dl, part, :], ctx, tp_at(dx, 0)
                )
        for dx in beside(nx):
            got[dx, dl, 1].wait_recv()

    def tp_opposite(got, dl):
        for dx in beside(nx):
            got[2, dl, dx].wait_recv()

    def z_begin(src, buf):
        got = {}
        for turn in range(2):
            for dz in beside(nz):
                part = halves(dz)[turn]
                got[dz, 0, turn] = remote(
                    src.at[part, :], buf.at[2 * dz, part, :], ctx_at(dz, 0, 0), tp
                )
        got[0, 1] = remote(src, buf.at[1], ctx_at(0, 0, 1), tp)
        return got

    def z_sides(buf, got):
        for dz in beside(nz):
            got[dz, 0, 0].wait_recv()
            if nz == 4:
                part = halves(dz)[0]
                got[2, 0, dz] = remote(
                    buf.at[2 * dz, part, :], buf.at[4, part, :], ctx_at(dz, 0, 0), tp
                )

    def z_rest(buf, got):
        for dz in beside(nz):
            got[dz, 0, 1].wait_recv()
            got[dz, 1] = remote(buf.at[2 * dz], buf.at[2 * dz + 1], ctx_at(0, 0, 1), tp)

    def z_opposite(buf, got):
        if nz == 4:
            for dz in beside(nz):
                got[2, 0, dz].wait_recv()
            got[2, 1] = remote(buf.at[4], buf.at[5], ctx_at(0, 0, 1), tp)

    got_x = tp_begin(x_in, xg)

    order = key_order(ny)
    place = {dy: p for p, dy in enumerate(order)}
    row_id = lax.broadcasted_iota(jnp.int32, (ROWS, HD), 0)
    lane_id = lax.broadcasted_iota(jnp.int32, (1, ROWS), 1)
    for p, dy in enumerate(order):
        at = ctx_at(0, ny - dy, 0)
        first, second = roster[2 * at] * BLOCK, roster[2 * at + 1] * BLOCK
        posk[p * ROWS:(p + 1) * ROWS, :] = row_id + jnp.where(row_id < BLOCK, first, second - BLOCK)
    for j in range(nj):
        at = ctx_at(nz - j // 2, 0, 2 - j % 2)
        first, second = roster[2 * at] * BLOCK, roster[2 * at + 1] * BLOCK
        posq[j:j + 1, :] = lane_id + jnp.where(lane_id < BLOCK, first, second - BLOCK)
    own = place[0]
    angle = posk[own * ROWS:(own + 1) * ROWS, :].astype(jnp.float32) * freq[...]
    cosine = jnp.cos(angle)
    lane = lax.broadcasted_iota(jnp.int32, (ROWS, HD), 1)
    sine = jnp.where(lane < HD // 2, -1.0, 1.0) * jnp.sin(angle)

    load_g.wait()
    load_o.wait()
    for h in range(GROUP):
        cols = slice(h * HD, (h + 1) * HD)
        product = gg[0, :, cols].astype(jnp.float32) * ol[:, cols].astype(jnp.float32)
        delta[0, :, cols] = jnp.sum(product.T, axis=0, keepdims=True)

    def project(dx, dl):
        at = ((xi + nx - dx) % nx) * nl + (zl + nl - dl) % nl
        rows = pl.ds(pl.multiple_of(at * WIDE, WIDE), WIDE)
        return matmul(xg[dx * nl + dl], wkv[rows, :])

    load_x.wait()
    load_wk.wait()
    load_wv.wait()
    raw = project(0, 0)

    if nl > 1:
        for turn in range(2):
            got_x[0, 1, turn].wait_send()
            sent.remove(got_x[0, 1, turn])
    got_q = z_begin(q_in, qg)
    tp_partner(xg, got_x)
    tp_sides(xg, got_x, 0)
    if nl > 1:
        raw += project(0, 1)
    for dx in beside(nx):
        raw += project(dx, 0)
    if nl > 1:
        tp_sides(xg, got_x, 1)
    z_sides(qg, got_q)
    if nl > 1:
        for dx in beside(nx):
            raw += project(dx, 1)
    if nx == 4:
        for dl in range(nl):
            tp_opposite(got_x, dl)
            raw += project(2, dl)

    key_raw = raw[:, 0:HD]
    keys = key_raw * cosine + pltpu.roll(key_raw, HD // 2, 1) * sine
    own_rows = pl.ds(own * ROWS, ROWS)
    kv[own_rows, 0:HD] = keys.astype(jnp.bfloat16)
    kv[own_rows, HD:2 * HD] = raw[:, HD:2 * HD].astype(jnp.bfloat16)

    def kv_send(dy_from, dy_to, start=0, count=ROWS):
        src = kv.at[pl.ds(place[dy_from] * ROWS + start, count), :]
        dst = kv.at[pl.ds(place[dy_to] * ROWS + start, count), :]
        return remote(src, dst, ctx_at(0, (ny + dy_to - dy_from) % ny, 0), tp)

    got_kv = {}
    for dy in direct:
        got_kv[dy] = [kv_send(0, dy)]
    z_rest(qg, got_q)
    got_g = z_begin(g_in, gg)
    got_delta = [
        remote(delta.at[0], delta.at[2 * dz + dc], ctx_at(dz, 0, dc), tp) for dz, dc in q_peers
    ]
    load_q.wait()

    def kv_forward():
        if ny == 8:
            got_kv[4] = []
            for dy, onward, start in ((2, 3, 0), (6, 5, ROWS // 2)):
                for copy in got_kv[dy]:
                    copy.wait_recv()
                got_kv[dy] = []
                got_kv[onward] = [kv_send(dy, onward)]
                got_kv[4].append(kv_send(dy, 4, start, ROWS // 2))

    def slot_of(a):
        return ((z + nz - a // 2) % nz) * 2 + (c + 2 - a % 2) % 2

    def place_of(j):
        return ((z + nz - j // 2) % nz) * 2 + (c + 2 - j % 2) % 2

    def score_step(k, a):
        j = slot_of(a)
        rows = pl.ds(pl.multiple_of(k * 2 * ROWS, 2 * ROWS), 2 * ROWS)
        scores = matmul_nt(kv[rows, 0:HD], stacked(qg[j]))
        allowed = posk[rows, :] <= posq[pl.ds(j, 1), :]
        for h in range(GROUP):
            cols = slice(h * HD, (h + 1) * HD)
            part = jnp.where(allowed, scores[:, cols] * (SCALE * LOG2E), NEG)
            top = jnp.maximum(jnp.max(part, axis=0, keepdims=True), FLOOR)
            weight = jnp.exp2(part - top)
            probs[k, j, :, cols] = weight
            peak[k, a, :, cols] = top
            total[k, a, :, cols] = jnp.sum(weight, axis=0, keepdims=True)

    batch = nj // 2

    def send_totals(b):
        for i in range(batch):
            a = b * batch + i
            top = peak[0, a]
            for k in range(1, chunks):
                top = jnp.maximum(top, peak[k, a])
            mass = total[0, a] * jnp.exp2(peak[0, a] - top)
            for k in range(1, chunks):
                mass += total[k, a] * jnp.exp2(peak[k, a] - top)
            lse_own[b, i:i + 1, :] = jnp.where(
                mass > 0.0, top + jnp.log(jnp.maximum(mass, 1e-30)) * LOG2E, NEG
            )
        return [
            remote(lse_own.at[b], lse_got.at[2 * dz + dc, b], ctx_at(dz, 0, dc), tp)
            for dz, dc in q_peers
        ]

    def take_totals(b, got):
        for copy in got:
            copy.wait_recv()
        top = lse_own[b]
        for s in range(1, nj):
            top = jnp.maximum(top, lse_got[s, b])
        mass = jnp.exp2(lse_own[b] - top)
        for s in range(1, nj):
            mass += jnp.exp2(lse_got[s, b] - top)
        lse = top + jnp.log(mass) * LOG2E
        for k in range(chunks):
            for i in range(batch):
                fac[k, b * batch + i] = jnp.exp2(peak[k, b * batch + i] - lse[i:i + 1, :])

    def each(count, step):
        unit = 4 if count % 4 == 0 else 1

        def run(i, carry):
            for u in range(unit):
                step(i * unit + u)
            return carry

        lax.fori_loop(0, count // unit, run, 0)

    mine = pl.ds(pl.multiple_of(c * HD, HD), HD)
    got_w = {}

    blocks = [(dx, dl) for dl in reversed(range(nl)) for dx in range(1, nx)]

    def send_weights():
        for dx, dl in blocks:
            rows = pl.ds(pl.multiple_of(tp_at(dx, dl) * WIDE, WIDE), WIDE)
            s = dx * nl + dl
            got_w[s] = remote(wkv.at[rows, mine], w_cols.at[s, :, mine], ctx, tp_at(dx, 0))

    got_w_sib = {}

    def share_weights():
        for s in got_w:
            got_w[s].wait_recv()
            got_w_sib[s] = remote(
                w_cols.at[s, :, mine], w_cols.at[s, :, mine], ctx_at(0, 0, 1), tp
            )

    def take_keys(k):
        for dy in order[2 * k:2 * k + 2]:
            for copy in got_kv.get(dy, []):
                copy.wait_recv()

    def scores_of(k, slots):
        for j in slots:
            score_step(k, place_of(j))

    late = [4, 5] if nz == 4 else []
    early = [j for j in range(nj) if j not in late]
    z_opposite(qg, got_q)
    got_q[0, 1].wait_recv()
    for dz in beside(nz):
        got_q[dz, 1].wait_recv()
    ahead_of_rest = [k for k in (chunks - 1, chunks - 2) if k > 0]
    if not ahead_of_rest:
        kv_forward()
    for k in ahead_of_rest:
        take_keys(k)
        scores_of(k, early)
        if k == chunks - 1:
            kv_forward()
            send_weights()
    z_sides(gg, got_g)
    if late:
        got_q[2, 1].wait_recv()
        for k in ahead_of_rest:
            scores_of(k, late)
    z_rest(gg, got_g)
    for k in reversed(range(1, max(chunks - 2, 1))):
        take_keys(k)
        each(nj, functools.partial(score_step, k))
    take_keys(0)
    if not ahead_of_rest:
        send_weights()
    got_lse = []
    for b in range(2):
        each(batch, lambda i, first=b * batch: score_step(0, first + i))
        got_lse.append(send_totals(b))
    z_opposite(gg, got_g)
    for k in range(chunks):
        rows = slice(2 * k * ROWS, 2 * (k + 1) * ROWS)
        kt[k] = kv[rows, 0:HD].astype(jnp.float32).T.astype(jnp.bfloat16)
    for copy in got_delta:
        copy.wait_recv()

    def first_d_probs(slots):
        def run(k, carry):
            rows = pl.ds(pl.multiple_of(k * 2 * ROWS, 2 * ROWS), 2 * ROWS)
            for j in slots:
                ahead[k, j] = matmul_nt(kv[rows, HD:2 * HD], stacked(gg[j])) - delta[j]
            return carry

        lax.fori_loop(0, chunks, run, 0)

    got_g[0, 1].wait_recv()
    for dz in beside(nz):
        got_g[dz, 1].wait_recv()
    first_d_probs(early)
    if late:
        got_g[2, 1].wait_recv()
        first_d_probs(late)
    take_totals(0, got_lse[0])

    got_dkv = {}
    got_sib = {}
    def both_cores(dz):
        got_sib[dz].wait_recv()
        return dqt[2 * dz] * SCALE + dq_sib[dz].astype(jnp.float32)

    got_half = {}
    def send_halves():
        if nz != 4:
            return
        dq_snd[2 * nz - 2] = both_cores(2).astype(jnp.bfloat16)
        got_half[1] = remote(dq_snd.at[2 * nz - 2, low, :], dq_half.at[low, :], ctx_at(3, 0, 0), tp)
        got_half[3] = remote(dq_snd.at[2 * nz - 2, high, :], dq_half.at[high, :], ctx_at(1, 0, 0), tp)

    got_relay = {}

    def dkv_send(dy, to, dst, start=0, count=ROWS):
        src = dkv_snd.at[place[dy], pl.ds(start, count), :]
        return remote(src, dst.at[pl.ds(start, count), :], ctx_at(0, (ny + to) % ny, 0), tp)

    def send_held():
        if ny != 8:
            return
        for i, (dy, half) in enumerate(((2, low), (6, high))):
            p = place[dy]
            got_relay[dy].wait_recv()
            got_relay[4, dy].wait_recv()
            part = held[i] + dkv_relay[i].astype(jnp.float32)
            rest = high if half is low else low
            dkv_snd[p, half, :] = (
                part[half] + dkv_relay[2, half, :].astype(jnp.float32)
            ).astype(jnp.bfloat16)
            dkv_snd[p, rest, :] = part[rest].astype(jnp.bfloat16)
            got_dkv[dy] = dkv_send(dy, -dy, dkv_got.at[p])

    for k in range(chunks):
        rows = slice(2 * k * ROWS, 2 * (k + 1) * ROWS)
        acc[...] = jnp.zeros_like(acc)

        def grad_step(j, k=k, rows=rows):
            gs, qs = stacked(gg[j]), stacked(qg[j])
            prob = probs[k, j] * fac[k, place_of(j)]
            d_scores = (prob * ahead[k, j]).astype(jnp.bfloat16)
            acc[:, HD:2 * HD] += matmul(prob.astype(jnp.bfloat16), gs)
            acc[:, 0:HD] += matmul(d_scores, qs)
            part = matmul(kt[k], d_scores)
            if k == 0:
                dqt[j] = part
            else:
                dqt[j] += part

        if k == 0:
            each(batch, lambda a, step=grad_step: step(slot_of(a)))
            take_totals(1, got_lse[1])
            each(batch, lambda a, step=grad_step: step(slot_of(batch + a)))
        if 0 < k < chunks - 1:
            each(nj, grad_step)
        if k == chunks - 1:
            for some in ((2,), (1, 3), (0,)):
                some = [dz for dz in some if dz < nz]
                for dz in some:
                    if k:
                        grad_step(2 * dz + 1)
                for dz in some:
                    dq_snd[dz] = (dqt[2 * dz + 1] * SCALE).astype(jnp.bfloat16)
                    got_sib[dz] = remote(dq_snd.at[dz], dq_sib.at[dz], ctx_at(0, 0, 1), tp)
                for dz in some:
                    if k:
                        grad_step(2 * dz)
                if (0 if nz == 1 else 1) in some:
                    send_held()
                    send_halves()
        for i, dy in enumerate(order[2 * k:2 * k + 2]):
            if dy == 0:
                continue
            p = 2 * k + i
            part = acc[i * ROWS:(i + 1) * ROWS, :]
            d_key, d_value = part[:, 0:HD] * SCALE, part[:, HD:2 * HD]
            if ny == 8 and dy in (2, 6):
                held[i, :, 0:HD] = d_key
                held[i, :, HD:2 * HD] = d_value
                continue
            dkv_snd[p, :, 0:HD] = d_key.astype(jnp.bfloat16)
            dkv_snd[p, :, HD:2 * HD] = d_value.astype(jnp.bfloat16)
            if ny == 8 and dy == 4:
                got_relay[4, 2] = dkv_send(4, -2, dkv_relay.at[2], 0, ROWS // 2)
                got_relay[4, 6] = dkv_send(4, 2, dkv_relay.at[2], ROWS // 2, ROWS // 2)
            elif ny == 8 and dy in (3, 5):
                side = 0 if dy == 3 else 1
                got_relay[2 if dy == 3 else 6] = dkv_send(dy, -1 if dy == 3 else 1, dkv_relay.at[side])
            else:
                got_dkv[dy] = dkv_send(dy, -dy, dkv_got.at[p])
        if k == max(chunks - 2, 0):
            share_weights()

    got_dq = {}
    for dz in beside(nz):
        both = both_cores(dz)
        if nz == 4:
            got_half[dz].wait_recv()
            part = low if dz == 1 else high
            other = high if dz == 1 else low
            dq_snd[nz + dz, part, :] = (
                both[part] + dq_half[part, :].astype(jnp.float32)
            ).astype(jnp.bfloat16)
            dq_snd[nz + dz, other, :] = both[other].astype(jnp.bfloat16)
        else:
            dq_snd[nz + dz] = both.astype(jnp.bfloat16)
        got_dq[dz] = remote(dq_snd.at[nz + dz], dq_got.at[dz], ctx_at(nz - dz, 0, 0), tp)

    i = own % 2
    d_key = acc[i * ROWS:(i + 1) * ROWS, 0:HD] * SCALE
    d_value = acc[i * ROWS:(i + 1) * ROWS, HD:2 * HD]
    for dy in got_dkv:
        got_dkv[dy].wait_recv()
        d_key += dkv_got[place[dy], :, 0:HD].astype(jnp.float32)
        d_value += dkv_got[place[dy], :, HD:2 * HD].astype(jnp.float32)
    d_key = d_key * cosine - pltpu.roll(d_key, HD // 2, 1) * sine
    d_kv = jnp.concatenate([d_key, d_value], axis=1).astype(jnp.bfloat16)
    dkv_all[0] = d_kv
    got_all = [
        remote(dkv_all.at[0], dkv_all.at[dx * nl], ctx, tp_at(dx, 0))
        for dx in beside(nx) + ([2] if nx == 4 else [])
    ]

    for copy in got_all[:2]:
        copy.wait_recv()
    for s in got_w_sib:
        got_w_sib[s].wait_recv()

    def term(dx, dl):
        if dx == 0:
            weights = wkv[pl.ds(pl.multiple_of(tp_at(0, dl) * WIDE, WIDE), WIDE), :]
        else:
            weights = w_cols[dx * nl + dl]
        return matmul_nt(dkv_all[dx * nl], weights).astype(jnp.bfloat16).astype(jnp.float32)

    def near_terms(dl):
        total = term(0, dl)
        for dx in beside(nx):
            total += term(dx, dl)
        return total

    sums = [near_terms(dl) for dl in reversed(range(nl))]
    for copy in got_all[2:]:
        copy.wait_recv()
    if nl > 1:
        di_snd[...] = (sums[0] + term(2, 1) if nx == 4 else sums[0]).astype(jnp.bfloat16)
        got_di = remote(di_snd, di_got, ctx, tp_at(0, 1))
    d_input = sums[-1] + term(2, 0) if nx == 4 else sums[-1]

    d_query = both_cores(0)
    for dz in beside(nz):
        got_dq[dz].wait_recv()
        d_query += dq_got[dz].astype(jnp.float32)
    for h in range(GROUP):
        cols = slice(h * HD, (h + 1) * HD)
        dq_out[:, cols] = d_query[:, cols].T.astype(jnp.bfloat16)

    if nl > 1:
        got_di.wait_recv()
        d_input += di_got[...].astype(jnp.float32)
    di_out[...] = d_input.astype(jnp.bfloat16)
    for copy in sent:
        copy.wait_send()


def body(grid, x_stash, w_key, w_value, query, out_stash, d_out, roster):
    nz, ny, nx, nl = grid
    nj, nt, chunks = 2 * nz, nx * nl, ny // 2
    bf16, f32 = jnp.bfloat16, jnp.float32
    half = ROPE_BASE ** (-(np.arange(HD // 2) * 2.0) / HD)
    freq = jnp.asarray(np.concatenate([half, half])[None, :].astype(np.float32))
    copies = 160
    vmem = pltpu.VMEM
    hbm = pl.BlockSpec(memory_space=pl.ANY)
    flops = 2 * nj * WIDE * ny * ROWS * HD * 5
    return pl.pallas_call(
        functools.partial(kernel, grid),
        out_shape=(vmem((ROWS, WIDE), bf16), vmem((ROWS, WIDE), bf16)),
        in_specs=[hbm] * 6
        + [pl.BlockSpec(memory_space=pltpu.SMEM), pl.BlockSpec(memory_space=pltpu.VMEM)],
        out_specs=(pl.BlockSpec(memory_space=vmem), pl.BlockSpec(memory_space=vmem)),
        scratch_shapes=[
            vmem((nt, ROWS, WIDE), bf16),
            vmem((nt * WIDE, 2 * HD), bf16),
            vmem((nj, ROWS, WIDE), bf16),
            vmem((nj, ROWS, WIDE), bf16),
            vmem((ROWS, WIDE), bf16),
            vmem((ny * ROWS, 2 * HD), bf16),
            vmem((chunks, HD, 2 * ROWS), bf16),
            vmem((ny * ROWS, HD), jnp.int32),
            vmem((nj, ROWS), jnp.int32),
            vmem((chunks, nj, 2 * ROWS, WIDE), f32),
            vmem((chunks, nj, 1, WIDE), f32),
            vmem((chunks, nj, 1, WIDE), f32),
            vmem((chunks, nj, 1, WIDE), f32),
            vmem((2, nz, WIDE), f32),
            vmem((nj, 2, nz, WIDE), f32),
            vmem((nj, 1, WIDE), f32),
            vmem((chunks, nj, 2 * ROWS, WIDE), f32),
            vmem((nj, HD, WIDE), f32),
            vmem((2 * nz, HD, WIDE), bf16),
            vmem((nz, HD, WIDE), bf16),
            vmem((HD, WIDE), bf16),
            vmem((nz, HD, WIDE), bf16),
            vmem((2 * ROWS, 2 * HD), f32),
            vmem((2, ROWS, 2 * HD), f32),
            vmem((ny, ROWS, 2 * HD), bf16),
            vmem((3, ROWS, 2 * HD), bf16),
            vmem((ny, ROWS, 2 * HD), bf16),
            vmem((nt, ROWS, 2 * HD), bf16),
            vmem((nt, WIDE, 2 * HD), bf16),
            vmem((ROWS, WIDE), bf16),
            vmem((ROWS, WIDE), bf16),
            pltpu.SemaphoreType.DMA((copies,)),
            pltpu.SemaphoreType.DMA((copies,)),
            pltpu.SemaphoreType.DMA((8,)),
        ],
        compiler_params=pltpu.CompilerParams(
            collective_id=0, has_side_effects=True, vmem_limit_bytes=56 * 1024 * 1024
        ),
        cost_estimate=pl.CostEstimate(
            flops=flops, bytes_accessed=4 * 1024 * 1024, transcendentals=nj * WIDE * ny * ROWS
        ),
    )(x_stash, w_key, w_value, query, out_stash, d_out, roster, freq)


def solution(mesh):
    grid = GRIDS[mesh.shape["ctx"], mesh.shape["tp"]]
    split = P("ctx", "tp")
    return jax.shard_map(
        functools.partial(body, grid),
        mesh=mesh,
        in_specs=(split, P(None, "tp"), P(None, "tp"), split, split, split, P()),
        out_specs=(split, split),
        check_vma=False,
    )
```

```python
import functools

import jax
import jax.numpy as jnp
import numpy as np
from jax import lax
from jax.experimental import pallas as pl
from jax.experimental.pallas import tpu as pltpu
from jax.sharding import PartitionSpec as P

HD = 128
GROUP = 4
BLOCK = 64
ROWS = 128
WIDE = GROUP * HD
ROPE_BASE = 500000.0
SCALE = HD ** -0.5
LOG2E = 1.4426950408889634
NEG = -1e30
FLOOR = -1e20

GRIDS = {(64, 8): (4, 8, 4, 2)}

NT = (((1,), (1,)), ((), ()))


def matmul_nt(a, b):
    return lax.dot_general(a, b, NT, preferred_element_type=jnp.float32)


def matmul(a, b):
    return jnp.dot(a, b, preferred_element_type=jnp.float32)


def stacked(block):
    return jnp.concatenate([block[:, h * HD:(h + 1) * HD] for h in range(GROUP)], axis=0)


def far_first(count):
    return sorted(range(count), key=lambda d: (-min(d, count - d), d))


def key_order(ny):
    return [4, 3, 5, 7, 2, 6, 1, 0] if ny == 8 else far_first(ny)


def beside(count):
    return sorted({1 % count, count - 1} - {0})


def kernel(
    grid, x_in, wk_in, wv_in, q_in, o_in, g_in, roster, freq,
    dq_out, di_out,
    xg, wkv, qg, gg, ol, kv, kt, posk, posq, probs, peak, total, fac, lse_own, lse_got,
    delta, ahead, dqt, dq_snd, dq_sib, dq_half, dq_got, acc, held, dkv_snd, dkv_relay, dkv_got, dkv_all, w_cols, di_snd, di_got,
    send_sem, recv_sem, local_sem,
):
    nz, ny, nx, nl = grid
    nj = 2 * nz
    chunks = ny // 2
    ctx, tp = lax.axis_index("ctx"), lax.axis_index("tp")
    z, y, c = ctx // (2 * ny), (ctx // 2) % ny, ctx % 2
    xi, zl = tp // nl, tp % nl

    def ctx_at(dz, dy, dc):
        return (((z + dz) % nz) * ny + (y + dy) % ny) * 2 + (c + dc) % 2

    def tp_at(dx, dl):
        return ((xi + dx) % nx) * nl + (zl + dl) % nl

    tp_peers = [(dx, 0) for dx in range(1, nx)] + [(0, dl) for dl in range(1, nl)]
    q_peers = [(dz, dc) for dz in range(nz) for dc in range(2) if (dz, dc) != (0, 0)]
    direct = [1, 7, 2, 6] if ny == 8 else list(range(1, ny))

    used = [0, 0]

    def local(src, dst):
        copy = pltpu.make_async_copy(src, dst, local_sem.at[used[0]])
        used[0] += 1
        copy.start()
        return copy

    sent = []

    def remote(src, dst, at_ctx, at_tp):
        i = used[1]
        used[1] += 1
        copy = pltpu.make_async_remote_copy(
            src_ref=src, dst_ref=dst, send_sem=send_sem.at[i], recv_sem=recv_sem.at[i],
            device_id=(at_ctx, at_tp), device_id_type=pl.DeviceIdType.MESH,
        )
        copy.start()
        sent.append(copy)
        return copy

    barrier = pltpu.get_barrier_semaphore()
    partners = [(ctx, tp_at(dx, dl)) for dx, dl in tp_peers]
    partners += [(ctx_at(dz, 0, dc), tp) for dz, dc in q_peers]
    partners += [(ctx_at(0, dy, 0), tp) for dy in direct]
    for partner in partners:
        pl.semaphore_signal(barrier, inc=1, device_id=partner, device_id_type=pl.DeviceIdType.MESH)

    load_x = local(x_in, xg.at[0])
    load_wk = local(wk_in, wkv.at[:, 0:HD])
    load_wv = local(wv_in, wkv.at[:, HD:2 * HD])
    load_g = local(g_in, gg.at[0])
    load_o = local(o_in, ol)
    load_q = local(q_in, qg.at[0])

    pl.semaphore_wait(barrier, len(partners))

    low, high = slice(0, ROWS // 2), slice(ROWS // 2, ROWS)

    def halves(step):
        return (low, high) if step == 1 else (high, low)

    def tp_round(src, buf, dl):
        got = {}
        for turn in range(2):
            for dx in beside(nx):
                part = halves(dx)[turn]
                got[dx, dl, turn] = remote(
                    src.at[part, :], buf.at[dx * nl + dl, part, :], ctx, tp_at(dx, 0)
                )
        return got

    def tp_begin(src, buf):
        got = {}
        if nl > 1:
            for turn, part in enumerate((low, high)):
                got[0, 1, turn] = remote(src.at[part, :], buf.at[1, part, :], ctx, tp_at(0, 1))
        got.update(tp_round(src, buf, 0))
        return got

    def tp_partner(buf, got):
        if nl > 1:
            for turn, part in enumerate((low, high)):
                got[0, 1, turn].wait_recv()
                for dx in beside(nx):
                    got[dx, 1, turn if halves(dx)[0] is low else 1 - turn] = remote(
                        buf.at[1, part, :], buf.at[dx * nl + 1, part, :], ctx, tp_at(dx, 0)
                    )

    def tp_sides(buf, got, dl):
        for dx in beside(nx):
            got[dx, dl, 0].wait_recv()
            if nx == 4:
                part = halves(dx)[0]
                got[2, dl, dx] = remote(
                    buf.at[dx * nl + dl, part, :], buf.at[2 * nl + dl, part, :], ctx, tp_at(dx, 0)
                )
        for dx in beside(nx):
            got[dx, dl, 1].wait_recv()

    def tp_opposite(got, dl):
        for dx in beside(nx):
            got[2, dl, dx].wait_recv()

    def z_begin(src, buf):
        got = {}
        for turn in range(2):
            for dz in beside(nz):
                part = halves(dz)[turn]
                got[dz, 0, turn] = remote(
                    src.at[part, :], buf.at[2 * dz, part, :], ctx_at(dz, 0, 0), tp
                )
        got[0, 1] = remote(src, buf.at[1], ctx_at(0, 0, 1), tp)
        return got

    def z_sides(buf, got):
        for dz in beside(nz):
            got[dz, 0, 0].wait_recv()
            if nz == 4:
                part = halves(dz)[0]
                got[2, 0, dz] = remote(
                    buf.at[2 * dz, part, :], buf.at[4, part, :], ctx_at(dz, 0, 0), tp
                )

    def z_rest(buf, got):
        for dz in beside(nz):
            got[dz, 0, 1].wait_recv()
            got[dz, 1] = remote(buf.at[2 * dz], buf.at[2 * dz + 1], ctx_at(0, 0, 1), tp)

    def z_opposite(buf, got):
        if nz == 4:
            for dz in beside(nz):
                got[2, 0, dz].wait_recv()
            got[2, 1] = remote(buf.at[4], buf.at[5], ctx_at(0, 0, 1), tp)

    got_x = tp_begin(x_in, xg)

    order = key_order(ny)
    place = {dy: p for p, dy in enumerate(order)}
    row_id = lax.broadcasted_iota(jnp.int32, (ROWS, HD), 0)
    lane_id = lax.broadcasted_iota(jnp.int32, (1, ROWS), 1)
    for p, dy in enumerate(order):
        at = ctx_at(0, ny - dy, 0)
        first, second = roster[2 * at] * BLOCK, roster[2 * at + 1] * BLOCK
        posk[p * ROWS:(p + 1) * ROWS, :] = row_id + jnp.where(row_id < BLOCK, first, second - BLOCK)
    for j in range(nj):
        at = ctx_at(nz - j // 2, 0, 2 - j % 2)
        first, second = roster[2 * at] * BLOCK, roster[2 * at + 1] * BLOCK
        posq[j:j + 1, :] = lane_id + jnp.where(lane_id < BLOCK, first, second - BLOCK)
    own = place[0]
    angle = posk[own * ROWS:(own + 1) * ROWS, :].astype(jnp.float32) * freq[...]
    cosine = jnp.cos(angle)
    lane = lax.broadcasted_iota(jnp.int32, (ROWS, HD), 1)
    sine = jnp.where(lane < HD // 2, -1.0, 1.0) * jnp.sin(angle)

    load_g.wait()
    load_o.wait()
    for h in range(GROUP):
        cols = slice(h * HD, (h + 1) * HD)
        product = gg[0, :, cols].astype(jnp.float32) * ol[:, cols].astype(jnp.float32)
        delta[0, :, cols] = jnp.sum(product.T, axis=0, keepdims=True)

    def project(dx, dl):
        at = ((xi + nx - dx) % nx) * nl + (zl + nl - dl) % nl
        rows = pl.ds(pl.multiple_of(at * WIDE, WIDE), WIDE)
        return matmul(xg[dx * nl + dl], wkv[rows, :])

    load_x.wait()
    load_wk.wait()
    load_wv.wait()
    raw = project(0, 0)

    if nl > 1:
        for turn in range(2):
            got_x[0, 1, turn].wait_send()
            sent.remove(got_x[0, 1, turn])
    got_q = z_begin(q_in, qg)
    tp_partner(xg, got_x)
    tp_sides(xg, got_x, 0)
    if nl > 1:
        raw += project(0, 1)
    for dx in beside(nx):
        raw += project(dx, 0)
    if nl > 1:
        tp_sides(xg, got_x, 1)
    z_sides(qg, got_q)
    if nl > 1:
        for dx in beside(nx):
            raw += project(dx, 1)
    if nx == 4:
        for dl in range(nl):
            tp_opposite(got_x, dl)
            raw += project(2, dl)

    key_raw = raw[:, 0:HD]
    keys = key_raw * cosine + pltpu.roll(key_raw, HD // 2, 1) * sine
    own_rows = pl.ds(own * ROWS, ROWS)
    kv[own_rows, 0:HD] = keys.astype(jnp.bfloat16)
    kv[own_rows, HD:2 * HD] = raw[:, HD:2 * HD].astype(jnp.bfloat16)

    def kv_send(dy_from, dy_to, start=0, count=ROWS):
        src = kv.at[pl.ds(place[dy_from] * ROWS + start, count), :]
        dst = kv.at[pl.ds(place[dy_to] * ROWS + start, count), :]
        return remote(src, dst, ctx_at(0, (ny + dy_to - dy_from) % ny, 0), tp)

    got_kv = {}
    for dy in direct:
        got_kv[dy] = [kv_send(0, dy)]
    z_rest(qg, got_q)
    got_g = z_begin(g_in, gg)
    got_delta = [
        remote(delta.at[0], delta.at[2 * dz + dc], ctx_at(dz, 0, dc), tp) for dz, dc in q_peers
    ]
    load_q.wait()

    def kv_forward():
        if ny == 8:
            got_kv[4] = []
            for dy, onward, start in ((2, 3, 0), (6, 5, ROWS // 2)):
                for copy in got_kv[dy]:
                    copy.wait_recv()
                got_kv[dy] = []
                got_kv[onward] = [kv_send(dy, onward)]
                got_kv[4].append(kv_send(dy, 4, start, ROWS // 2))

    def slot_of(a):
        return ((z + nz - a // 2) % nz) * 2 + (c + 2 - a % 2) % 2

    def place_of(j):
        return ((z + nz - j // 2) % nz) * 2 + (c + 2 - j % 2) % 2

    def score_step(k, a):
        j = slot_of(a)
        rows = pl.ds(pl.multiple_of(k * 2 * ROWS, 2 * ROWS), 2 * ROWS)
        scores = matmul_nt(kv[rows, 0:HD], stacked(qg[j]))
        allowed = posk[rows, :] <= posq[pl.ds(j, 1), :]
        for h in range(GROUP):
            cols = slice(h * HD, (h + 1) * HD)
            part = jnp.where(allowed, scores[:, cols] * (SCALE * LOG2E), NEG)
            top = jnp.maximum(jnp.max(part, axis=0, keepdims=True), FLOOR)
            weight = jnp.exp2(part - top)
            probs[k, j, :, cols] = weight
            peak[k, a, :, cols] = top
            total[k, a, :, cols] = jnp.sum(weight, axis=0, keepdims=True)

    batch = nj // 2

    def send_totals(b):
        for i in range(batch):
            a = b * batch + i
            top = peak[0, a]
            for k in range(1, chunks):
                top = jnp.maximum(top, peak[k, a])
            mass = total[0, a] * jnp.exp2(peak[0, a] - top)
            for k in range(1, chunks):
                mass += total[k, a] * jnp.exp2(peak[k, a] - top)
            lse_own[b, i:i + 1, :] = jnp.where(
                mass > 0.0, top + jnp.log(jnp.maximum(mass, 1e-30)) * LOG2E, NEG
            )
        return [
            remote(lse_own.at[b], lse_got.at[2 * dz + dc, b], ctx_at(dz, 0, dc), tp)
            for dz, dc in q_peers
        ]

    def take_totals(b, got):
        for copy in got:
            copy.wait_recv()
        top = lse_own[b]
        for s in range(1, nj):
            top = jnp.maximum(top, lse_got[s, b])
        mass = jnp.exp2(lse_own[b] - top)
        for s in range(1, nj):
            mass += jnp.exp2(lse_got[s, b] - top)
        lse = top + jnp.log(mass) * LOG2E
        for k in range(chunks):
            for i in range(batch):
                fac[k, b * batch + i] = jnp.exp2(peak[k, b * batch + i] - lse[i:i + 1, :])

    def each(count, step):
        unit = next(u for u in (8, 4, 1) if count % u == 0)

        def run(i, carry):
            for u in range(unit):
                step(i * unit + u)
            return carry

        lax.fori_loop(0, count // unit, run, 0)

    mine = pl.ds(pl.multiple_of(c * HD, HD), HD)
    got_w = {}

    blocks = [(dx, dl) for dl in reversed(range(nl)) for dx in range(1, nx)]

    def send_weights():
        for dx, dl in blocks:
            rows = pl.ds(pl.multiple_of(tp_at(dx, dl) * WIDE, WIDE), WIDE)
            s = dx * nl + dl
            got_w[s] = remote(wkv.at[rows, mine], w_cols.at[s, :, mine], ctx, tp_at(dx, 0))

    got_w_sib = {}

    def share_weights():
        for s in got_w:
            got_w[s].wait_recv()
            got_w_sib[s] = remote(
                w_cols.at[s, :, mine], w_cols.at[s, :, mine], ctx_at(0, 0, 1), tp
            )

    def take_keys(k):
        for dy in order[2 * k:2 * k + 2]:
            for copy in got_kv.get(dy, []):
                copy.wait_recv()

    def scores_of(k, slots):
        for j in slots:
            score_step(k, place_of(j))

    late = [4, 5] if nz == 4 else []
    early = [j for j in range(nj) if j not in late]
    z_opposite(qg, got_q)
    got_q[0, 1].wait_recv()
    for dz in beside(nz):
        got_q[dz, 1].wait_recv()
    ahead_of_rest = [k for k in (chunks - 1, chunks - 2) if k > 0]
    if not ahead_of_rest:
        kv_forward()
    for k in ahead_of_rest:
        take_keys(k)
        scores_of(k, early)
        if k == chunks - 1:
            kv_forward()
            send_weights()
    z_sides(gg, got_g)
    if late:
        got_q[2, 1].wait_recv()
        for k in ahead_of_rest:
            scores_of(k, late)
    z_rest(gg, got_g)
    for k in reversed(range(1, max(chunks - 2, 1))):
        take_keys(k)
        each(nj, functools.partial(score_step, k))
    take_keys(0)
    if not ahead_of_rest:
        send_weights()
    got_lse = []
    for b in range(2):
        each(batch, lambda i, first=b * batch: score_step(0, first + i))
        got_lse.append(send_totals(b))
    z_opposite(gg, got_g)
    for k in range(chunks):
        rows = slice(2 * k * ROWS, 2 * (k + 1) * ROWS)
        kt[k] = kv[rows, 0:HD].astype(jnp.float32).T.astype(jnp.bfloat16)
    for copy in got_delta:
        copy.wait_recv()

    def first_d_probs(slots):
        def run(k, carry):
            rows = pl.ds(pl.multiple_of(k * 2 * ROWS, 2 * ROWS), 2 * ROWS)
            for j in slots:
                ahead[k, j] = matmul_nt(kv[rows, HD:2 * HD], stacked(gg[j])) - delta[j]
            return carry

        lax.fori_loop(0, chunks, run, 0)

    got_g[0, 1].wait_recv()
    for dz in beside(nz):
        got_g[dz, 1].wait_recv()
    first_d_probs(early)
    if late:
        got_g[2, 1].wait_recv()
        first_d_probs(late)
    take_totals(0, got_lse[0])

    got_dkv = {}
    got_sib = {}
    def both_cores(dz):
        got_sib[dz].wait_recv()
        return dqt[2 * dz] * SCALE + dq_sib[dz].astype(jnp.float32)

    got_half = {}
    def send_halves():
        if nz != 4:
            return
        dq_snd[2 * nz - 2] = both_cores(2).astype(jnp.bfloat16)
        got_half[1] = remote(dq_snd.at[2 * nz - 2, low, :], dq_half.at[low, :], ctx_at(3, 0, 0), tp)
        got_half[3] = remote(dq_snd.at[2 * nz - 2, high, :], dq_half.at[high, :], ctx_at(1, 0, 0), tp)

    got_relay = {}

    def dkv_send(dy, to, dst, start=0, count=ROWS):
        src = dkv_snd.at[place[dy], pl.ds(start, count), :]
        return remote(src, dst.at[pl.ds(start, count), :], ctx_at(0, (ny + to) % ny, 0), tp)

    def send_held():
        if ny != 8:
            return
        for i, (dy, half) in enumerate(((2, low), (6, high))):
            p = place[dy]
            got_relay[dy].wait_recv()
            got_relay[4, dy].wait_recv()
            part = held[i] + dkv_relay[i].astype(jnp.float32)
            rest = high if half is low else low
            dkv_snd[p, half, :] = (
                part[half] + dkv_relay[2, half, :].astype(jnp.float32)
            ).astype(jnp.bfloat16)
            dkv_snd[p, rest, :] = part[rest].astype(jnp.bfloat16)
            got_dkv[dy] = dkv_send(dy, -dy, dkv_got.at[p])

    for k in range(chunks):
        rows = slice(2 * k * ROWS, 2 * (k + 1) * ROWS)
        acc[...] = jnp.zeros_like(acc)

        def grad_step(j, k=k, rows=rows):
            gs, qs = stacked(gg[j]), stacked(qg[j])
            prob = probs[k, j] * fac[k, place_of(j)]
            d_scores = (prob * ahead[k, j]).astype(jnp.bfloat16)
            acc[:, HD:2 * HD] += matmul(prob.astype(jnp.bfloat16), gs)
            acc[:, 0:HD] += matmul(d_scores, qs)
            part = matmul(kt[k], d_scores)
            if k == 0:
                dqt[j] = part
            else:
                dqt[j] += part

        if k == 0:
            take_totals(1, got_lse[1])
        if k < chunks - 1 or k == 0:
            each(nj, grad_step)
        if k == chunks - 1:
            for some in ((2,), (1, 3), (0,)):
                some = [dz for dz in some if dz < nz]
                for dz in some:
                    if k:
                        grad_step(2 * dz + 1)
                for dz in some:
                    dq_snd[dz] = (dqt[2 * dz + 1] * SCALE).astype(jnp.bfloat16)
                    got_sib[dz] = remote(dq_snd.at[dz], dq_sib.at[dz], ctx_at(0, 0, 1), tp)
                for dz in some:
                    if k:
                        grad_step(2 * dz)
                if (0 if nz == 1 else 1) in some:
                    send_held()
                    send_halves()
        for i, dy in enumerate(order[2 * k:2 * k + 2]):
            if dy == 0:
                continue
            p = 2 * k + i
            part = acc[i * ROWS:(i + 1) * ROWS, :]
            d_key, d_value = part[:, 0:HD] * SCALE, part[:, HD:2 * HD]
            if ny == 8 and dy in (2, 6):
                held[i, :, 0:HD] = d_key
                held[i, :, HD:2 * HD] = d_value
                continue
            dkv_snd[p, :, 0:HD] = d_key.astype(jnp.bfloat16)
            dkv_snd[p, :, HD:2 * HD] = d_value.astype(jnp.bfloat16)
            if ny == 8 and dy == 4:
                got_relay[4, 2] = dkv_send(4, -2, dkv_relay.at[2], 0, ROWS // 2)
                got_relay[4, 6] = dkv_send(4, 2, dkv_relay.at[2], ROWS // 2, ROWS // 2)
            elif ny == 8 and dy in (3, 5):
                side = 0 if dy == 3 else 1
                got_relay[2 if dy == 3 else 6] = dkv_send(dy, -1 if dy == 3 else 1, dkv_relay.at[side])
            else:
                got_dkv[dy] = dkv_send(dy, -dy, dkv_got.at[p])
        if k == max(chunks - 2, 0):
            share_weights()

    got_dq = {}
    for dz in beside(nz):
        both = both_cores(dz)
        if nz == 4:
            got_half[dz].wait_recv()
            part = low if dz == 1 else high
            other = high if dz == 1 else low
            dq_snd[nz + dz, part, :] = (
                both[part] + dq_half[part, :].astype(jnp.float32)
            ).astype(jnp.bfloat16)
            dq_snd[nz + dz, other, :] = both[other].astype(jnp.bfloat16)
        else:
            dq_snd[nz + dz] = both.astype(jnp.bfloat16)
        got_dq[dz] = remote(dq_snd.at[nz + dz], dq_got.at[dz], ctx_at(nz - dz, 0, 0), tp)

    i = own % 2
    d_key = acc[i * ROWS:(i + 1) * ROWS, 0:HD] * SCALE
    d_value = acc[i * ROWS:(i + 1) * ROWS, HD:2 * HD]
    for dy in got_dkv:
        got_dkv[dy].wait_recv()
        d_key += dkv_got[place[dy], :, 0:HD].astype(jnp.float32)
        d_value += dkv_got[place[dy], :, HD:2 * HD].astype(jnp.float32)
    d_key = d_key * cosine - pltpu.roll(d_key, HD // 2, 1) * sine
    d_kv = jnp.concatenate([d_key, d_value], axis=1).astype(jnp.bfloat16)
    dkv_all[0] = d_kv
    got_all = [
        remote(dkv_all.at[0], dkv_all.at[dx * nl], ctx, tp_at(dx, 0))
        for dx in beside(nx) + ([2] if nx == 4 else [])
    ]

    for copy in got_all[:2]:
        copy.wait_recv()
    for s in got_w_sib:
        got_w_sib[s].wait_recv()

    def term(dx, dl):
        if dx == 0:
            weights = wkv[pl.ds(pl.multiple_of(tp_at(0, dl) * WIDE, WIDE), WIDE), :]
        else:
            weights = w_cols[dx * nl + dl]
        return matmul_nt(dkv_all[dx * nl], weights).astype(jnp.bfloat16).astype(jnp.float32)

    def near_terms(dl):
        total = term(0, dl)
        for dx in beside(nx):
            total += term(dx, dl)
        return total

    sums = [near_terms(dl) for dl in reversed(range(nl))]
    for copy in got_all[2:]:
        copy.wait_recv()
    if nl > 1:
        di_snd[...] = (sums[0] + term(2, 1) if nx == 4 else sums[0]).astype(jnp.bfloat16)
        got_di = remote(di_snd, di_got, ctx, tp_at(0, 1))
    d_input = sums[-1] + term(2, 0) if nx == 4 else sums[-1]

    d_query = both_cores(0)
    for dz in beside(nz):
        got_dq[dz].wait_recv()
        d_query += dq_got[dz].astype(jnp.float32)
    for h in range(GROUP):
        cols = slice(h * HD, (h + 1) * HD)
        dq_out[:, cols] = d_query[:, cols].T.astype(jnp.bfloat16)

    if nl > 1:
        got_di.wait_recv()
        d_input += di_got[...].astype(jnp.float32)
    di_out[...] = d_input.astype(jnp.bfloat16)
    for copy in sent:
        copy.wait_send()


def body(grid, x_stash, w_key, w_value, query, out_stash, d_out, roster):
    nz, ny, nx, nl = grid
    nj, nt, chunks = 2 * nz, nx * nl, ny // 2
    bf16, f32 = jnp.bfloat16, jnp.float32
    half = ROPE_BASE ** (-(np.arange(HD // 2) * 2.0) / HD)
    freq = jnp.asarray(np.concatenate([half, half])[None, :].astype(np.float32))
    copies = 160
    vmem = pltpu.VMEM
    hbm = pl.BlockSpec(memory_space=pl.ANY)
    flops = 2 * nj * WIDE * ny * ROWS * HD * 5
    return pl.pallas_call(
        functools.partial(kernel, grid),
        out_shape=(vmem((ROWS, WIDE), bf16), vmem((ROWS, WIDE), bf16)),
        in_specs=[hbm] * 6
        + [pl.BlockSpec(memory_space=pltpu.SMEM), pl.BlockSpec(memory_space=pltpu.VMEM)],
        out_specs=(pl.BlockSpec(memory_space=vmem), pl.BlockSpec(memory_space=vmem)),
        scratch_shapes=[
            vmem((nt, ROWS, WIDE), bf16),
            vmem((nt * WIDE, 2 * HD), bf16),
            vmem((nj, ROWS, WIDE), bf16),
            vmem((nj, ROWS, WIDE), bf16),
            vmem((ROWS, WIDE), bf16),
            vmem((ny * ROWS, 2 * HD), bf16),
            vmem((chunks, HD, 2 * ROWS), bf16),
            vmem((ny * ROWS, HD), jnp.int32),
            vmem((nj, ROWS), jnp.int32),
            vmem((chunks, nj, 2 * ROWS, WIDE), f32),
            vmem((chunks, nj, 1, WIDE), f32),
            vmem((chunks, nj, 1, WIDE), f32),
            vmem((chunks, nj, 1, WIDE), f32),
            vmem((2, nz, WIDE), f32),
            vmem((nj, 2, nz, WIDE), f32),
            vmem((nj, 1, WIDE), f32),
            vmem((chunks, nj, 2 * ROWS, WIDE), f32),
            vmem((nj, HD, WIDE), f32),
            vmem((2 * nz, HD, WIDE), bf16),
            vmem((nz, HD, WIDE), bf16),
            vmem((HD, WIDE), bf16),
            vmem((nz, HD, WIDE), bf16),
            vmem((2 * ROWS, 2 * HD), f32),
            vmem((2, ROWS, 2 * HD), f32),
            vmem((ny, ROWS, 2 * HD), bf16),
            vmem((3, ROWS, 2 * HD), bf16),
            vmem((ny, ROWS, 2 * HD), bf16),
            vmem((nt, ROWS, 2 * HD), bf16),
            vmem((nt, WIDE, 2 * HD), bf16),
            vmem((ROWS, WIDE), bf16),
            vmem((ROWS, WIDE), bf16),
            pltpu.SemaphoreType.DMA((copies,)),
            pltpu.SemaphoreType.DMA((copies,)),
            pltpu.SemaphoreType.DMA((8,)),
        ],
        compiler_params=pltpu.CompilerParams(
            collective_id=0, has_side_effects=True, vmem_limit_bytes=56 * 1024 * 1024
        ),
        cost_estimate=pl.CostEstimate(
            flops=flops, bytes_accessed=4 * 1024 * 1024, transcendentals=nj * WIDE * ny * ROWS
        ),
    )(x_stash, w_key, w_value, query, out_stash, d_out, roster, freq)


def solution(mesh):
    grid = GRIDS[mesh.shape["ctx"], mesh.shape["tp"]]
    split = P("ctx", "tp")
    return jax.shard_map(
        functools.partial(body, grid),
        mesh=mesh,
        in_specs=(split, P(None, "tp"), P(None, "tp"), split, split, split, P()),
        out_specs=(split, split),
        check_vma=False,
    )
```
